512 devices in a mesh: dp: 32 (over z, core), seq: 16 (over y, x).
Axes of the slice: x: 4, y: 4, z: 16, core: 2. Of those that a mesh axis runs over, the one named last changes fastest.
Arguments:
- tokens: bfloat16 [32, 64, 64, 1152], P('dp', None, 'seq'), may hold values from -6 to 6
- slot_owner: int32 [32, 64], P('dp'), may hold values from 0 to 31, as said below
- clip_pieces: int32 [32, 4, 16], P('dp'), may hold values from 0 to 63, as said below
- clip_length: int32 [32, 4], P('dp'), may hold values from 256 to 1024, as said below
- modulation: bfloat16 [32, 4, 3, 1152], P('dp'), may hold values from -4 to 4
- qkv_weight: bfloat16 [1152, 3, 1152], P(None, None, 'seq'), may hold values from -0.1875 to 0.1875
- qk_gain: float32 [2, 72], replicated, may hold values from 0.1 to 1.9
- proj_weight: bfloat16 [1152, 1152], P('seq'), may hold values from -0.1875 to 0.1875
Outputs:
- block_output: bfloat16 [32, 64, 64, 1152], P('dp', None, 'seq')
The draws below stay inside these ranges and needn't reach their ends.
Inputs may be any that keep to these rules, and one draw needn't show every extreme that they name: `slot_owner`: each row names every owner exactly 2 times. `clip_pieces`: each owner's table holds every arrival index 0 to 63 exactly once. `clip_length`: every owner has one clip of 1024 tokens.
All inputs are finite; a program needn't handle non-finite values.
Results may differ from the reference program's by a relative error of at most 0.0045.
Values may be sent and summed in bfloat16 or wider, within the bound.
A program may use at most 64 MiB of HBM per device.

```python
import math
import jax
import jax.numpy as jnp
from jax import lax

D = 1152
HEADS = 16
HD = 72
PIECES_DEV = 64
PIECES = 16
PEER_PIECES = 2
CLIPS_OWN = 4
PIECE_TOK = 64
CLIP_TOK = 1024
N_DP = 32


def draw_slot_owner(key, part):
    key = jax.random.fold_in(key, 11)
    repeated = jnp.repeat(jnp.arange(N_DP, dtype=jnp.int32), PIECES_DEV // N_DP)
    row_keys = jax.random.split(key, N_DP)
    shuffled = jax.vmap(lambda row_key: jax.random.permutation(row_key, repeated))(row_keys)
    return shuffled.astype(jnp.int32)


def draw_clip_pieces(key, part):
    key = jax.random.fold_in(key, 12)
    numbers = jnp.arange(PIECES_DEV, dtype=jnp.int32)
    row_keys = jax.random.split(key, N_DP)
    shuffled = jax.vmap(lambda row_key: jax.random.permutation(row_key, numbers))(row_keys)
    return shuffled.reshape(N_DP, CLIPS_OWN, PIECES).astype(jnp.int32)


def draw_clip_length(key, part):
    key = jax.random.fold_in(key, 13)
    first_key, second_key = jax.random.split(key)
    drawn = jax.random.randint(first_key, (N_DP, CLIPS_OWN), CLIP_TOK // 4, CLIP_TOK + 1, dtype=jnp.int32)
    longest = jax.random.randint(second_key, (N_DP, 1), 0, CLIPS_OWN, dtype=jnp.int32)
    column = jnp.arange(CLIPS_OWN, dtype=jnp.int32)[None, :]
    return jnp.where(column == longest, CLIP_TOK, drawn).astype(jnp.int32)


def block_levels(own_key, dims, shards, least, high):
    def one(position, shards_of):
        heights = jax.random.uniform(jax.random.fold_in(jax.random.fold_in(own_key, 6), position), (shards_of,), jnp.float32, least / len(shards), high / len(shards))
        return jnp.repeat(jnp.exp(heights), dims[position] // shards_of).reshape((-1,) + (1,) * (len(dims) - position - 1))

    factor_of = one(*shards[0])
    for cut in shards[1:]:
        factor_of = factor_of * one(*cut)
    return factor_of


def noise(stream_key, extent, deviation, limit, cuts=(), held_as=jnp.bfloat16):
    values = jax.random.normal(stream_key, extent, jnp.float32) * deviation
    if len(cuts) > 0:
        values = block_levels(stream_key, extent, cuts, -0.22, 0.18) * values
    return jnp.clip(values, min=-limit, max=limit).astype(held_as)


def setup_inputs(seed: int = 0) -> dict:
    key_of = jax.random.split(jax.random.key(seed), 9)
    return {
        "tokens": noise(key_of[0], (N_DP, PIECES_DEV, PIECE_TOK, D), 1.0, 6.0, ((0, 32), (2, 16))),
        "slot_owner": draw_slot_owner(jax.random.fold_in(key_of[8], 71), 0),
        "clip_pieces": draw_clip_pieces(jax.random.fold_in(key_of[8], 71), 0),
        "clip_length": draw_clip_length(jax.random.fold_in(key_of[8], 71), 0),
        "modulation": noise(key_of[4], (N_DP, CLIPS_OWN, 3, D), 1.0, 4.0, ((0, 32),)),
        "qkv_weight": noise(key_of[5], (D, 3, HEADS * HD), D ** -0.5, 0.1875, ((2, 16),)),
        "qk_gain": jnp.clip(1.0 + 0.18 * jax.random.normal(key_of[6], (2, HD), jnp.float32), 0.1, 1.9),
        "proj_weight": noise(key_of[7], (HEADS * HD, D), (HEADS * HD) ** -0.5, 0.1875, ((0, 16),)),
    }


EPSILON = 1e-06

def scaled_norm(head_block, gain_row):
    mean_square = lax.optimization_barrier(jnp.mean(head_block * head_block, axis=-1, keepdims=True))
    return (head_block * lax.rsqrt(mean_square + EPSILON) * gain_row.astype(jnp.float32)).astype(jnp.bfloat16)

def attend_owner(operands, qkv_weight, qk_gain, proj_weight):
    received, piece_table, lengths, modulation = operands
    clip_rows = received[piece_table.reshape(-1)].reshape(CLIPS_OWN, CLIP_TOK, D)
    clip_float = clip_rows.astype(jnp.float32)
    average = lax.optimization_barrier(jnp.mean(clip_float, axis=-1, keepdims=True))
    centered = clip_float - average
    variance = lax.optimization_barrier(jnp.mean(centered * centered, axis=-1, keepdims=True))
    normed = centered * lax.rsqrt(variance + EPSILON)
    factors = modulation.astype(jnp.float32)
    hidden = (normed * (1.0 + factors[:, 1][:, None, :]) + factors[:, 0][:, None, :]).astype(jnp.bfloat16)
    projected = jnp.dot(hidden.reshape(-1, D), qkv_weight.reshape(D, -1), preferred_element_type=jnp.float32)
    projected = projected.reshape(CLIPS_OWN, CLIP_TOK, 3, HEADS, HD)
    queries = scaled_norm(projected[:, :, 0], qk_gain[0])
    keys_part = scaled_norm(projected[:, :, 1], qk_gain[1])
    values = projected[:, :, 2].astype(jnp.bfloat16)
    scores = jnp.einsum('cqhe,ckhe->chqk', queries.astype(jnp.float32), keys_part.astype(jnp.float32)) * (1.0 / math.sqrt(HD))
    positions = jnp.arange(CLIP_TOK, dtype=jnp.int32)
    in_clip = positions[None, :] < lengths[:, None]
    unscaled = jnp.where(in_clip[:, None, None, :], jnp.exp(scores), 0.0)
    weights = (unscaled / lax.optimization_barrier(jnp.sum(unscaled, axis=-1, keepdims=True))).astype(jnp.bfloat16)
    attended = jnp.einsum('chqk,ckhe->cqhe', weights.astype(jnp.float32), values.astype(jnp.float32)).astype(jnp.bfloat16)
    branch = jnp.dot(attended.reshape(-1, HEADS * HD), proj_weight, preferred_element_type=jnp.float32)
    branch = branch.reshape(CLIPS_OWN, CLIP_TOK, D)
    result = jnp.where(in_clip[:, :, None], clip_float + factors[:, 2][:, None, :] * branch, 0.0).astype(jnp.bfloat16)
    flattened = result.reshape(PIECES_DEV, PIECE_TOK, D)
    inverse = jnp.argsort(piece_table.reshape(-1)).astype(jnp.int32)
    return flattened[inverse]

def reference(tokens, slot_owner, clip_pieces, clip_length, modulation, qkv_weight, qk_gain, proj_weight):
    sorted_slots = jnp.argsort(slot_owner, axis=1, stable=True).astype(jnp.int32)
    sources = jnp.repeat(jnp.arange(N_DP, dtype=jnp.int32), PEER_PIECES)
    arrivals = jnp.tile(jnp.arange(PEER_PIECES, dtype=jnp.int32), N_DP)
    owners = jnp.arange(N_DP, dtype=jnp.int32)
    chosen = sorted_slots[sources[None, :], owners[:, None] * PEER_PIECES + arrivals[None, :]]
    received = tokens[sources[None, :], chosen]
    returned = lax.map(lambda operands: attend_owner(operands, qkv_weight, qk_gain, proj_weight), (received, clip_pieces, clip_length, modulation))
    slot_ranks = jnp.argsort(sorted_slots, axis=1).astype(jnp.int32)
    places = owners[:, None] * PEER_PIECES + slot_ranks - slot_owner * PEER_PIECES
    return returned[slot_owner, places]
```

```python
import math

import jax
import jax.numpy as jnp
from jax import lax
from jax.experimental import pallas as pl
from jax.experimental.pallas import tpu as pltpu
from jax.sharding import PartitionSpec as P

MESH = pl.DeviceIdType.MESH
F32 = jnp.float32
BF16 = jnp.bfloat16
I32 = jnp.int32
D = 1152
HD = 72
N_DP = 32
N_SEQ = 16
NX = 4
NY = 4
CLIPS = 4
HALF = 640
REST = D - HALF
CHUNKS = 4
PER_CHUNK = N_DP // CHUNKS
ROWS = 256
CHUNK_ROWS = ROWS // CHUNKS
EPSILON = 1e-06


def iota(shape, dim):
    return lax.broadcasted_iota(I32, shape, dim)


def mm(a, b):
    return lax.dot_general(a, b, (((1,), (0,)), ((), ())), preferred_element_type=F32)


def mm_nt(a, b):
    return lax.dot_general(a, b, (((1,), (1,)), ((), ())), preferred_element_type=F32)


def slot_of(distance):
    return jnp.where(distance < 16, 2 * (16 - distance) - 1, 2 * (distance - 16))


def distance_of(slot):
    k = (slot + 1) // 2
    return 16 + k * (1 - 2 * (slot % 2))


def column_of(row, n):
    spread = jnp.broadcast_to(row.astype(F32), (n, n))
    picked = jnp.where(iota((n, n), 0) == iota((n, n), 1), spread, 0.0)
    return jnp.sum(picked, axis=1, keepdims=True).astype(I32)


def kernel(
    tok, owner, table, length, mod, w, gain, pw, out,
    outgoing, arrived, hid, wall, wcat, res, pwall, pwcat, stage, qkv, qc, kc, vc, att, attsend, attin,
    ret, back, spread, spread_t, unroute, route, clip_col,
    dp_send, dp_recv, y_send, y_recv, x_send, x_recv, w_send, w_recv, wf_send, wf_recv,
    p_send, p_recv, pf_send, pf_recv, a_send, a_recv, r_send, r_recv, local, x_local,
):
    me = lax.axis_index("dp")
    sq = lax.axis_index("seq")
    core = me % 2
    sibling = me + 1 - 2 * core
    y = sq // NX
    x = sq % NX

    def remote(src, dst, send, recv, dp, seq):
        return pltpu.make_async_remote_copy(
            src_ref=src, dst_ref=dst, send_sem=send, recv_sem=recv,
            device_id={"dp": dp, "seq": seq}, device_id_type=MESH,
        )

    def tok_out(i):
        return remote(outgoing.at[i], arrived.at[i], dp_send.at[i], dp_recv.at[i], (me + distance_of(i)) % N_DP, sq)

    def ret_out(i):
        return remote(
            ret.at[i], back.at[i], r_send.at[i], r_recv.at[i], (me - distance_of(i) + N_DP) % N_DP, sq
        )

    def hid_copy(k, step, row):
        return remote(
            hid.at[k, row], hid.at[k, row], y_send.at[k, step], y_recv.at[k, step], me, ((y + step) % NY) * NX + x
        )

    def w_copy(step, col):
        return remote(
            wall.at[col, core], wall.at[col, core], w_send.at[step], w_recv.at[step], me, y * NX + (x + step) % NX
        )

    def w_forward(step, half):
        col = (x - step + NX) % NX
        return remote(wall.at[col, half], wall.at[col, half], wf_send.at[step], wf_recv.at[step], sibling, sq)

    def x_copy(k, step, col):
        return remote(
            stage.at[k, (x + step) % NX], qkv.at[col, k], x_send.at[k, step], x_recv.at[k, step],
            me, y * NX + (x + step) % NX,
        )

    def p_copy(step, head):
        return remote(
            pwall.at[core, head], pwall.at[core, head], p_send.at[step], p_recv.at[step], me, (sq + step) % N_SEQ
        )

    def p_forward(step, half):
        head = (sq - step + N_SEQ) % N_SEQ
        return remote(pwall.at[half, head], pwall.at[half, head], pf_send.at[step], pf_recv.at[step], sibling, sq)

    def a_copy(step, head):
        to = (sq + step) % N_SEQ
        return remote(attsend.at[to], attin.at[head], a_send.at[step], a_recv.at[step], me, to)

    def each(first, last, action):
        lax.fori_loop(first, last, lambda i, c: (action(i), c)[1], 0)

    barrier = pltpu.get_barrier_semaphore()
    each(1, N_DP, lambda i: pl.semaphore_signal(
        barrier, inc=1, device_id={"dp": (me + i) % N_DP, "seq": sq}, device_id_type=MESH))
    each(1, N_SEQ, lambda i: pl.semaphore_signal(
        barrier, inc=1, device_id={"dp": me, "seq": (sq + i) % N_SEQ}, device_id_type=MESH))

    own = []
    for half in range(2):
        cols = pl.ds(half * REST, HALF)
        own.append(pltpu.make_async_copy(w.at[:, :, cols], wall.at[x, half], local.at[half]))
        own.append(pltpu.make_async_copy(pw.at[:, cols], pwall.at[half, sq], local.at[2 + half]))
    for copy in own:
        copy.start()

    owners = owner[...]
    owners_f = jnp.broadcast_to(owners.astype(F32), (64, 64))
    owners_col = column_of(owners, 64).astype(F32)
    earlier = (owners_col == owners_f) & (iota((64, 64), 0) < iota((64, 64), 1))
    rank = jnp.sum(jnp.where(earlier, 1.0, 0.0), axis=0, keepdims=True).astype(I32)
    piece_key = slot_of((owners - me + N_DP) & (N_DP - 1)) * 8 + rank * 4
    widen = jnp.where((iota((64, ROWS), 1) >> 2) == iota((64, ROWS), 0), 1.0, 0.0).astype(BF16)
    keys = mm(jnp.broadcast_to(piece_key.astype(F32), (16, 64)).astype(BF16), widen)[0:1].astype(I32)
    keys = keys + (iota((1, ROWS), 1) & 3)
    route_rows = jnp.where(iota((ROWS, ROWS), 0) == keys, 1.0, 0.0).astype(BF16)
    outgoing[...] = mm(route_rows, tok[...]).reshape(N_DP, 8, D).astype(BF16)

    pl.semaphore_wait(barrier, N_DP - 1 + N_SEQ - 1)

    own[0].wait()
    own[2].wait()
    for step in (2, 1, 3):
        w_copy(step, x).start()
    each(0, N_DP - 1, lambda i: tok_out(i).start())
    self_in = pltpu.make_async_copy(outgoing.at[N_DP - 1], arrived.at[N_DP - 1], local.at[4])
    self_in.start()

    keys_col = column_of(keys, ROWS)
    route[...] = jnp.where(iota((ROWS, ROWS), 1) == keys_col, 1.0, 0.0).astype(BF16)

    def arrival_row(pieces, row):
        source, rank_of = pieces >> 1, pieces & 1
        return slot_of((me - source + N_DP) & (N_DP - 1)) * 8 + rank_of * 4 + row

    def table_row(width, clip_shift):
        lane = iota((16, width), 1)
        pick = jnp.where(((lane >> 2) & 15) == iota((16, width), 0), 1.0, 0.0).astype(BF16)
        wide = mm(table[...].astype(F32).astype(BF16), pick)
        mine = (iota((CLIPS, width), 1) >> clip_shift) == iota((CLIPS, width), 0)
        pieces = jnp.sum(jnp.where(mine, wide, 0.0), axis=0, keepdims=True).astype(I32)
        return arrival_row(pieces, iota((1, width), 1) & 3)

    key_short = table_row(ROWS, 6)
    of_clip = iota((ROWS, ROWS), 0) == key_short
    unroute[...] = jnp.where(of_clip, 1.0, 0.0).astype(BF16)
    place = jnp.sum(jnp.where(of_clip, iota((ROWS, ROWS), 1).astype(F32), 0.0), axis=1, keepdims=True)
    clip_col[...] = jnp.broadcast_to(place.astype(I32), (ROWS, 128))
    key_long = table_row(2 * ROWS, 7)
    wide_lane = iota((1, 2 * ROWS), 1)
    key_long = (key_long >> 6) * 128 + ((wide_lane >> 6) & 1) * 64 + (key_long & 63)
    spread[...] = jnp.where(iota((512, 512), 0) == key_long, 1.0, 0.0).astype(BF16)
    spread_t[...] = jnp.where(iota((512, 512), 1) == column_of(key_long, 512), 1.0, 0.0).astype(BF16)

    def of_its_clip(clip, which):
        factors = mod[which].astype(F32)
        rows = [factors[c:c + 1, :] for c in range(CLIPS)]
        return jnp.where(clip == 0, rows[0], jnp.where(clip == 1, rows[1], jnp.where(clip == 2, rows[2], rows[3])))

    def chunk_in(k, last):
        def wait(i):
            tok_out(i).wait_recv()
        each(k * PER_CHUNK, (k + 1) * PER_CHUNK - (1 if last else 0), wait)
        if last:
            self_in.wait()
        rows = arrived[pl.ds(k * PER_CHUNK, PER_CHUNK)].astype(F32).reshape(CHUNK_ROWS, D)
        clip = clip_col[pl.ds(pl.multiple_of(k * CHUNK_ROWS, CHUNK_ROWS), CHUNK_ROWS), 0:1] >> 6
        centered = rows - jnp.mean(rows, axis=-1, keepdims=True)
        variance = jnp.mean(centered * centered, axis=-1, keepdims=True)
        normed = centered * lax.rsqrt(variance + EPSILON)
        hidden = normed * (1.0 + of_its_clip(clip, 1)) + of_its_clip(clip, 0)
        hid[k, pl.ds(y, 1)] = hidden.astype(BF16)[None]
        for step in (2, 1, 3):
            hid_copy(k, step, y).start()

    gains = []
    for i in range(2):
        spread_gain = jnp.broadcast_to(gain[i:i + 1, :], (HD, HD))
        picked = jnp.where(iota((HD, HD), 0) == iota((HD, HD), 1), spread_gain, 0.0)
        gains.append(jnp.sum(picked, axis=1, keepdims=True))

    def own_stage(k):
        return pltpu.make_async_copy(stage.at[k, x], qkv.at[x, k], x_local.at[k])

    def chunk_qkv(k):
        for step in (1, 2, 3):
            hid_copy(k, step, (y - step + NY) % NY).wait_recv()
        rows = hid[k].reshape(ROWS, D)
        res[...] = mm_nt(wcat[...], rows)
        for head in range(NX):
            base = head * 3 * HD
            for part in range(2):
                block = res[base + part * HD:base + (part + 1) * HD, :]
                mean_square = jnp.mean(block * block, axis=0, keepdims=True)
                stage[k, head, part] = (block * lax.rsqrt(mean_square + EPSILON) * gains[part]).astype(BF16)
            stage[k, head, 2] = res[base + 2 * HD:base + 3 * HD, :].astype(BF16)
        for step in (2, 1, 3):
            x_copy(k, step, x).start()
        own_stage(k).start()

    chunk_in(0, False)
    for step in (1, 2, 3):
        w_copy(step, (x - step + NX) % NX).wait_recv()
        w_forward(step, core).start()
    chunk_in(1, False)
    for step in (1, 2, 3):
        w_forward(step, 1 - core).wait_recv()
    for pair in range(NX // 2):
        rows = slice(pair * 6 * HD, (pair + 1) * 6 * HD)
        cols = slice(2 * pair, 2 * pair + 2)
        wcat[rows, 0:HALF] = wall[cols, 0].astype(F32).reshape(6 * HD, HALF).astype(BF16)
        wcat[rows, HALF:D] = wall[cols, 1].astype(F32).reshape(6 * HD, HALF)[:, HALF - REST:].astype(BF16)
    chunk_qkv(0)
    chunk_in(2, False)
    chunk_qkv(1)
    chunk_in(3, True)
    chunk_qkv(2)
    chunk_qkv(3)

    own[1].wait()
    own[3].wait()
    each(1, N_SEQ, lambda i: p_copy(i, sq).start())

    for k in range(CHUNKS):
        own_stage(k).wait()
        for step in (1, 2, 3):
            x_copy(k, step, (x - step + NX) % NX).wait_recv()
    lane = iota((1, 128), 1)

    def to_clips(col, carry):
        for pair in range(2):
            def part_of(part):
                blocks = [qkv[col, k, part, :, pair * 128:(pair + 1) * 128] for k in range(CHUNKS)]
                return jnp.concatenate(blocks, axis=1)
            queries = mm(part_of(0), spread[...]).astype(BF16)
            keys_of = mm_nt(spread_t[...], part_of(1)).astype(BF16)
            values = mm(part_of(2), spread[...])
            for clip in range(CLIPS):
                cut = slice(clip * 128, (clip + 1) * 128)
                qc[clip, col * 2 + pair] = queries[:, cut]
                kc[clip, col * 2 + pair] = keys_of[cut, :]
                position = ((lane >> 2) & 15) * 64 + ((pair * 2 + (lane >> 6)) * NX + col) * 4 + (lane & 3)
                inside = jnp.where(position < length[0, clip], 1.0, 0.0)
                ones = jnp.broadcast_to(inside, (8, 128))
                vc[clip, col * 2 + pair] = jnp.concatenate([values[:, cut] * inside, ones], axis=0).astype(BF16)
        return carry

    lax.fori_loop(0, NX, to_clips, 0)

    factor = math.log2(math.e) / math.sqrt(HD)

    def attend(clip, carry):
        keys_of = kc[clip].reshape(8 * 128, HD)
        values = jnp.concatenate([vc[clip, j] for j in range(8)], axis=1)
        for block in range(4):
            queries = jnp.concatenate([qc[clip, 2 * block], qc[clip, 2 * block + 1]], axis=1)
            scores = mm(keys_of, queries)
            unscaled = jnp.exp2(scores * factor).astype(BF16)
            summed = mm(values, unscaled)
            attended = (summed[0:HD] / summed[HD:HD + 1]).astype(BF16)
            att[clip, 2 * block] = attended[:, 0:128]
            att[clip, 2 * block + 1] = attended[:, 128:256]
        return carry

    lax.fori_loop(0, 2, attend, 0)
    each(1, N_SEQ, lambda i: p_copy(i, (sq - i + N_SEQ) % N_SEQ).wait_recv())
    each(1, N_SEQ, lambda i: p_forward(i, core).start())
    lax.fori_loop(2, CLIPS, attend, 0)

    come = iota((512, 512), 0)
    go = iota((512, 512), 1)
    swap = jnp.where(come == ((go >> 6) & 3) * 128 + (go >> 8) * 64 + (go & 63), 1.0, 0.0).astype(BF16)
    for pair in range(8):
        blocks = jnp.concatenate([att[clip, pair] for clip in range(CLIPS)], axis=1)
        swapped = mm(blocks, swap).astype(BF16)
        for half in range(2):
            attsend[((pair % 2) * 2 + half) * NX + pair // 2] = swapped[:, half * ROWS:(half + 1) * ROWS]
    each(1, N_SEQ, lambda i: a_copy(i, sq).start())
    self_att = pltpu.make_async_copy(attsend.at[sq], attin.at[sq], local.at[5])
    self_att.start()

    each(1, N_SEQ, lambda i: p_forward(i, 1 - core).wait_recv())
    for head in range(N_SEQ // 2):
        rows = pl.ds(head * 2 * HD, 2 * HD)
        pwcat[rows, 0:HALF] = pwall[0, 2 * head:2 * head + 2].astype(F32).reshape(2 * HD, HALF).astype(BF16)
        pwcat[rows, HALF:D] = (
            pwall[1, 2 * head:2 * head + 2].astype(F32).reshape(2 * HD, HALF)[:, HALF - REST:].astype(BF16))

    self_att.wait()
    each(1, N_SEQ, lambda i: a_copy(i, (sq - i + N_SEQ) % N_SEQ).wait_recv())
    heads = attin[...].astype(F32).reshape(N_SEQ * HD, ROWS).astype(BF16)
    for part in range(2):
        half_rows = ROWS // 2
        cut = slice(part * half_rows, (part + 1) * half_rows)
        joined = mm_nt(unroute[cut, :], heads).astype(BF16)
        branch = mm(joined, pwcat[...])
        where = clip_col[cut, 0:1]
        clip = where >> 6
        position = ((where >> 2) & 15) * 64 + sq * 4 + (where & 3)
        limit = jnp.where(clip == 0, length[0, 0], jnp.where(
            clip == 1, length[0, 1], jnp.where(clip == 2, length[0, 2], length[0, 3])))
        rows = arrived[part * 16:(part + 1) * 16].astype(F32).reshape(half_rows, D)
        result = jnp.where(position < limit, rows + of_its_clip(clip, 2) * branch, 0.0)
        ret[part * 16:(part + 1) * 16] = result.reshape(16, 8, D).astype(BF16)
        each(part * 16, part * 16 + 16 - part, lambda i: ret_out(i).start())
    self_back = pltpu.make_async_copy(ret.at[N_DP - 1], back.at[N_DP - 1], local.at[6])
    self_back.start()

    for step in (1, 2, 3):
        w_copy(step, x).wait_send()
        w_forward(step, core).wait_send()
        for k in range(CHUNKS):
            hid_copy(k, step, y).wait_send()
            x_copy(k, step, x).wait_send()
    each(0, N_DP - 1, lambda i: tok_out(i).wait_send())
    each(1, N_SEQ, lambda i: p_copy(i, sq).wait_send())
    each(1, N_SEQ, lambda i: p_forward(i, core).wait_send())
    each(1, N_SEQ, lambda i: a_copy(i, sq).wait_send())

    self_back.wait()
    each(0, N_DP - 1, lambda i: ret_out(i).wait_recv())
    returned = back[...].astype(F32).reshape(ROWS, D).astype(BF16)
    out[...] = mm(route[...], returned).astype(BF16)
    each(0, N_DP - 1, lambda i: ret_out(i).wait_send())


def body(tokens, slot_owner, clip_pieces, clip_length, modulation, qkv_weight, qk_gain, proj_weight):
    vmem = pl.BlockSpec(memory_space=pltpu.VMEM)
    smem = pl.BlockSpec(memory_space=pltpu.SMEM)
    dma = pltpu.SemaphoreType.DMA
    result = pl.pallas_call(
        kernel,
        out_shape=jax.ShapeDtypeStruct((ROWS, D), BF16),
        in_specs=[vmem, vmem, vmem, smem, vmem, vmem, vmem, vmem],
        out_specs=vmem,
        scratch_shapes=[
            pltpu.VMEM((N_DP, 8, D), BF16),
            pltpu.VMEM((N_DP, 8, D), BF16),
            pltpu.VMEM((CHUNKS, NY, CHUNK_ROWS, D), BF16),
            pltpu.VMEM((NX, 2, 3, HD, HALF), BF16),
            pltpu.VMEM((NX * 3 * HD, D), BF16),
            pltpu.VMEM((NX * 3 * HD, ROWS), F32),
            pltpu.VMEM((2, N_SEQ, HD, HALF), BF16),
            pltpu.VMEM((N_SEQ * HD, D), BF16),
            pltpu.VMEM((CHUNKS, NX, 3, HD, ROWS), BF16),
            pltpu.VMEM((NX, CHUNKS, 3, HD, ROWS), BF16),
            pltpu.VMEM((CLIPS, 8, HD, 128), BF16),
            pltpu.VMEM((CLIPS, 8, 128, HD), BF16),
            pltpu.VMEM((CLIPS, 8, HD + 8, 128), BF16),
            pltpu.VMEM((CLIPS, 8, HD, 128), BF16),
            pltpu.VMEM((N_SEQ, HD, ROWS), BF16),
            pltpu.VMEM((N_SEQ, HD, ROWS), BF16),
            pltpu.VMEM((N_DP, 8, D), BF16),
            pltpu.VMEM((N_DP, 8, D), BF16),
            pltpu.VMEM((512, 512), BF16),
            pltpu.VMEM((512, 512), BF16),
            pltpu.VMEM((ROWS, ROWS), BF16),
            pltpu.VMEM((ROWS, ROWS), BF16),
            pltpu.VMEM((ROWS, 128), I32),
            dma((N_DP,)), dma((N_DP,)),
            dma((CHUNKS, 4)), dma((CHUNKS, 4)), dma((CHUNKS, 4)), dma((CHUNKS, 4)),
            dma((4,)), dma((4,)), dma((4,)), dma((4,)),
            dma((N_SEQ,)), dma((N_SEQ,)), dma((N_SEQ,)), dma((N_SEQ,)), dma((N_SEQ,)), dma((N_SEQ,)),
            dma((N_DP,)), dma((N_DP,)),
            dma((8,)), dma((CHUNKS,)),
        ],
        compiler_params=pltpu.CompilerParams(
            collective_id=0, has_side_effects=True, vmem_limit_bytes=50 * 1024 * 1024
        ),
        cost_estimate=pl.CostEstimate(flops=5 * 10**9, bytes_accessed=4 * 10**6, transcendentals=4 * 10**6),
        name="block",
    )(
        tokens[0].reshape(ROWS, D),
        slot_owner,
        clip_pieces[0],
        clip_length,
        modulation[0].transpose(1, 0, 2),
        qkv_weight.transpose(1, 2, 0),
        qk_gain,
        proj_weight,
    )
    return result.reshape(1, 64, 4, D)


def solution(mesh):
    return jax.shard_map(
        body,
        mesh=mesh,
        in_specs=(
            P("dp", None, "seq", None),
            P("dp", None),
            P("dp", None, None),
            P("dp", None),
            P("dp", None, None, None),
            P(None, None, "seq"),
            P(),
            P("seq", None),
        ),
        out_specs=P("dp", None, "seq", None),
        check_vma=False,
    )
```

```python
import math

import jax
import jax.numpy as jnp
from jax import lax
from jax.experimental import pallas as pl
from jax.experimental.pallas import tpu as pltpu
from jax.sharding import PartitionSpec as P

MESH = pl.DeviceIdType.MESH
F32 = jnp.float32
BF16 = jnp.bfloat16
I32 = jnp.int32
D = 1152
HD = 72
N_DP = 32
N_SEQ = 16
NX = 4
NY = 4
CLIPS = 4
HALF = 640
REST = D - HALF
CHUNKS = 4
PER_CHUNK = N_DP // CHUNKS
ROWS = 256
CHUNK_ROWS = ROWS // CHUNKS
EPSILON = 1e-06


def iota(shape, dim):
    return lax.broadcasted_iota(I32, shape, dim)


def mm(a, b):
    return lax.dot_general(a, b, (((1,), (0,)), ((), ())), preferred_element_type=F32)


def mm_nt(a, b):
    return lax.dot_general(a, b, (((1,), (1,)), ((), ())), preferred_element_type=F32)


def slot_of(distance):
    return (distance & (CHUNKS - 1)) * PER_CHUNK + (distance >> 2)


def distance_of(slot):
    return (slot % PER_CHUNK) * CHUNKS + slot // PER_CHUNK


def column_of(row, n):
    spread = jnp.broadcast_to(row.astype(F32), (n, n))
    picked = jnp.where(iota((n, n), 0) == iota((n, n), 1), spread, 0.0)
    return jnp.sum(picked, axis=1, keepdims=True).astype(I32)


def kernel(
    tok, owner, table, length, mod, w, gain, pw, out,
    outgoing, arrived, hid, wall, wcat, res, pwall, pwcat, stage, qkv, qc, kc, vc, att, attsend, attin,
    ret, back, spread, spread_t, unroute, route, clip_col,
    dp_send, dp_recv, y_send, y_recv, x_send, x_recv, w_send, w_recv,
    p_send, p_recv, pf_send, pf_recv, a_send, a_recv, r_send, r_recv, local, x_local,
):
    me = lax.axis_index("dp")
    sq = lax.axis_index("seq")
    core = me % 2
    sibling = me + 1 - 2 * core
    u = (sq // NX) * (1 - core) + (sq % NX) * core
    v = (sq % NX) * (1 - core) + (sq // NX) * core

    def seq_at(u_of, v_of):
        return (u_of * 4 + v_of) * (1 - core) + (v_of * 4 + u_of) * core

    def ahead(position, step):
        return (position + step) % 4

    def behind(position, step):
        return (position - step + 4) % 4

    def remote(src, dst, send, recv, dp, seq):
        return pltpu.make_async_remote_copy(
            src_ref=src, dst_ref=dst, send_sem=send, recv_sem=recv,
            device_id={"dp": dp, "seq": seq}, device_id_type=MESH,
        )

    def tok_out(i):
        return remote(outgoing.at[i], arrived.at[i], dp_send.at[i], dp_recv.at[i], (me + distance_of(i)) % N_DP, sq)

    def ret_out(i):
        return remote(
            ret.at[i], back.at[i], r_send.at[i], r_recv.at[i], (me - distance_of(i) + N_DP) % N_DP, sq
        )

    def hid_copy(k, step, row):
        return remote(
            hid.at[k, row], hid.at[k, row], y_send.at[k, step], y_recv.at[k, step], me, seq_at(ahead(u, step), v)
        )

    def w_copy(step, col):
        return remote(wall.at[col], wall.at[col], w_send.at[step], w_recv.at[step], me, seq_at(u, ahead(v, step)))

    def x_copy(k, step, col):
        return remote(
            stage.at[k, ahead(v, step)], qkv.at[col, k], x_send.at[k, step], x_recv.at[k, step],
            me, seq_at(u, ahead(v, step)),
        )

    def p_first(step, col):
        return remote(
            pwall.at[core, u, col], pwall.at[core, u, col], p_send.at[0, step], p_recv.at[0, step],
            me, seq_at(u, ahead(v, step)),
        )

    def p_second(step, row):
        return remote(
            pwall.at[core, row], pwall.at[core, row], p_send.at[1, step], p_recv.at[1, step],
            me, seq_at(ahead(u, step), v),
        )

    def p_forward(row, half):
        return remote(pwall.at[half, row], pwall.at[half, row], pf_send.at[row], pf_recv.at[row], sibling, sq)

    def a_copy(step, head):
        to = (sq + step) % N_SEQ
        at = to * (1 - core) + ((to % 4) * 4 + to // 4) * core
        return remote(attsend.at[at], attin.at[head], a_send.at[step], a_recv.at[step], me, to)

    def each(first, last, action):
        lax.fori_loop(first, last, lambda i, c: (action(i), c)[1], 0)

    barrier = pltpu.get_barrier_semaphore()
    each(1, N_DP, lambda i: pl.semaphore_signal(
        barrier, inc=1, device_id={"dp": (me + i) % N_DP, "seq": sq}, device_id_type=MESH))
    each(1, N_SEQ, lambda i: pl.semaphore_signal(
        barrier, inc=1, device_id={"dp": me, "seq": (sq + i) % N_SEQ}, device_id_type=MESH))

    cols = pl.ds(pl.multiple_of(core * REST, 128), HALF)
    own_w = pltpu.make_async_copy(w, wall.at[v], local.at[0])
    own_p = pltpu.make_async_copy(pw.at[:, cols], pwall.at[core, u, v], local.at[1])
    own_w.start()
    own_p.start()

    owners = owner[...]
    owners_f = jnp.broadcast_to(owners.astype(F32), (64, 64))
    owners_col = column_of(owners, 64).astype(F32)
    earlier = (owners_col == owners_f) & (iota((64, 64), 0) < iota((64, 64), 1))
    rank = jnp.sum(jnp.where(earlier, 1.0, 0.0), axis=0, keepdims=True).astype(I32)
    piece_key = slot_of((owners - me + N_DP) & (N_DP - 1)) * 8 + rank * 4
    widen = jnp.where((iota((64, ROWS), 1) >> 2) == iota((64, ROWS), 0), 1.0, 0.0).astype(BF16)
    keys = mm(jnp.broadcast_to(piece_key.astype(F32), (16, 64)).astype(BF16), widen)[0:1].astype(I32)
    keys = keys + (iota((1, ROWS), 1) & 3)
    route_rows = jnp.where(iota((ROWS, ROWS), 0) == keys, 1.0, 0.0).astype(BF16)
    outgoing[...] = mm(route_rows, tok[...]).reshape(N_DP, 8, D).astype(BF16)

    pl.semaphore_wait(barrier, N_DP - 1 + N_SEQ - 1)

    own_w.wait()
    own_p.wait()
    self_in = pltpu.make_async_copy(outgoing.at[0], arrived.at[0], local.at[4])
    self_in.start()

    def tokens_out(k):
        each(k * PER_CHUNK + (1 if k == 0 else 0), (k + 1) * PER_CHUNK, lambda i: tok_out(i).start())

    tokens_out(0)
    for step in (2, 1, 3):
        w_copy(step, v).start()
    tokens_out(1)
    for step in (2, 1, 3):
        p_first(step, v).start()

    keys_col = column_of(keys, ROWS)
    route[...] = jnp.where(iota((ROWS, ROWS), 1) == keys_col, 1.0, 0.0).astype(BF16)

    def arrival_row(pieces, row):
        source, rank_of = pieces >> 1, pieces & 1
        return slot_of((me - source + N_DP) & (N_DP - 1)) * 8 + rank_of * 4 + row

    def table_row(width, clip_shift):
        lane = iota((16, width), 1)
        pick = jnp.where(((lane >> 2) & 15) == iota((16, width), 0), 1.0, 0.0).astype(BF16)
        wide = mm(table[...].astype(F32).astype(BF16), pick)
        mine = (iota((CLIPS, width), 1) >> clip_shift) == iota((CLIPS, width), 0)
        pieces = jnp.sum(jnp.where(mine, wide, 0.0), axis=0, keepdims=True).astype(I32)
        return arrival_row(pieces, iota((1, width), 1) & 3)

    key_short = table_row(ROWS, 6)
    of_clip = iota((ROWS, ROWS), 0) == key_short
    unroute[...] = jnp.where(of_clip, 1.0, 0.0).astype(BF16)
    place = jnp.sum(jnp.where(of_clip, iota((ROWS, ROWS), 1).astype(F32), 0.0), axis=1, keepdims=True)
    clip_col[...] = jnp.broadcast_to(place.astype(I32), (ROWS, 128))
    key_long = table_row(2 * ROWS, 7)
    wide_lane = iota((1, 2 * ROWS), 1)
    key_long = (key_long >> 6) * 128 + ((wide_lane >> 6) & 1) * 64 + (key_long & 63)
    spread[...] = jnp.where(iota((512, 512), 0) == key_long, 1.0, 0.0).astype(BF16)
    spread_t[...] = jnp.where(iota((512, 512), 1) == column_of(key_long, 512), 1.0, 0.0).astype(BF16)

    def of_its_clip(clip, which):
        factors = mod[which].astype(F32)
        rows = [factors[c:c + 1, :] for c in range(CLIPS)]
        return jnp.where(clip == 0, rows[0], jnp.where(clip == 1, rows[1], jnp.where(clip == 2, rows[2], rows[3])))

    def chunk_in(k):
        if k == 0:
            self_in.wait()
        each(k * PER_CHUNK + (1 if k == 0 else 0), (k + 1) * PER_CHUNK, lambda i: tok_out(i).wait_recv())
        if k + 2 < CHUNKS:
            tokens_out(k + 2)
        rows = arrived[pl.ds(k * PER_CHUNK, PER_CHUNK)].astype(F32).reshape(CHUNK_ROWS, D)
        clip = clip_col[pl.ds(pl.multiple_of(k * CHUNK_ROWS, CHUNK_ROWS), CHUNK_ROWS), 0:1] >> 6
        centered = rows - jnp.mean(rows, axis=-1, keepdims=True)
        variance = jnp.mean(centered * centered, axis=-1, keepdims=True)
        normed = centered * lax.rsqrt(variance + EPSILON)
        hidden = normed * (1.0 + of_its_clip(clip, 1)) + of_its_clip(clip, 0)
        hid[k, pl.ds(u, 1)] = hidden.astype(BF16)[None]
        for step in (2, 1, 3):
            hid_copy(k, step, u).start()

    gains = []
    for i in range(2):
        spread_gain = jnp.broadcast_to(gain[i:i + 1, :], (HD, HD))
        picked = jnp.where(iota((HD, HD), 0) == iota((HD, HD), 1), spread_gain, 0.0)
        gains.append(jnp.sum(picked, axis=1, keepdims=True))

    def own_stage(k):
        return pltpu.make_async_copy(stage.at[k, v], qkv.at[v, k], x_local.at[k])

    def chunk_qkv(k):
        for step in (1, 2, 3):
            hid_copy(k, step, behind(u, step)).wait_recv()
        rows = hid[k].reshape(ROWS, D)
        res[...] = mm_nt(wcat[...], rows)
        for head in range(NX):
            base = head * 3 * HD
            for part in range(2):
                block = res[base + part * HD:base + (part + 1) * HD, :]
                mean_square = jnp.mean(block * block, axis=0, keepdims=True)
                stage[k, head, part] = (block * lax.rsqrt(mean_square + EPSILON) * gains[part]).astype(BF16)
            stage[k, head, 2] = res[base + 2 * HD:base + 3 * HD, :].astype(BF16)
        for step in (2, 1, 3):
            x_copy(k, step, v).start()
        own_stage(k).start()

    chunk_in(0)
    chunk_in(1)
    for step in (1, 2, 3):
        w_copy(step, behind(v, step)).wait_recv()
    for pair in range(2):
        rows = wall[2 * pair:2 * pair + 2].astype(F32).reshape(6 * HD, D)
        wcat[pair * 6 * HD:(pair + 1) * 6 * HD, :] = rows.astype(BF16)
    chunk_qkv(0)
    chunk_in(2)
    chunk_qkv(1)
    chunk_in(3)
    chunk_qkv(2)
    chunk_qkv(3)

    for step in (1, 2, 3):
        p_first(step, behind(v, step)).wait_recv()
    for step in (2, 1, 3):
        p_second(step, u).start()

    for k in range(CHUNKS):
        own_stage(k).wait()
        for step in (1, 2, 3):
            x_copy(k, step, behind(v, step)).wait_recv()
    lane = iota((1, 128), 1)

    def to_clips(col, carry):
        for pair in range(2):
            def part_of(part):
                blocks = [qkv[col, k, part, :, pair * 128:(pair + 1) * 128] for k in range(CHUNKS)]
                return jnp.concatenate(blocks, axis=1)
            queries = mm(part_of(0), spread[...]).astype(BF16)
            keys_of = mm_nt(spread_t[...], part_of(1)).astype(BF16)
            values = mm(part_of(2), spread[...])
            for clip in range(CLIPS):
                cut = slice(clip * 128, (clip + 1) * 128)
                qc[clip, col * 2 + pair] = queries[:, cut]
                kc[clip, col * 2 + pair] = keys_of[cut, :]
                holder = jnp.where(lane < 64, seq_at(pair * 2, col), seq_at(pair * 2 + 1, col))
                position = ((lane >> 2) & 15) * 64 + holder * 4 + (lane & 3)
                inside = jnp.where(position < length[0, clip], 1.0, 0.0)
                ones = jnp.broadcast_to(inside, (8, 128))
                vc[clip, col * 2 + pair] = jnp.concatenate([values[:, cut] * inside, ones], axis=0).astype(BF16)
        return carry

    lax.fori_loop(0, NX, to_clips, 0)

    factor = math.log2(math.e) / math.sqrt(HD)

    def attend(clip, carry):
        keys_of = kc[clip].reshape(8 * 128, HD)
        values = jnp.concatenate([vc[clip, j] for j in range(8)], axis=1)
        for block in range(4):
            queries = jnp.concatenate([qc[clip, 2 * block], qc[clip, 2 * block + 1]], axis=1)
            scores = mm(keys_of, queries)
            unscaled = jnp.exp2(scores * factor).astype(BF16)
            summed = mm(values, unscaled)
            attended = (summed[0:HD] / summed[HD:HD + 1]).astype(BF16)
            att[clip, 2 * block] = attended[:, 0:128]
            att[clip, 2 * block + 1] = attended[:, 128:256]
        return carry

    lax.fori_loop(0, 3, attend, 0)
    for step in (1, 2, 3):
        p_second(step, behind(u, step)).wait_recv()
    each(0, 4, lambda i: p_forward(i, core).start())
    lax.fori_loop(3, CLIPS, attend, 0)

    come = iota((512, 512), 0)
    go = iota((512, 512), 1)
    swap = jnp.where(come == ((go >> 6) & 3) * 128 + (go >> 8) * 64 + (go & 63), 1.0, 0.0).astype(BF16)
    for pair in range(8):
        blocks = jnp.concatenate([att[clip, pair] for clip in range(CLIPS)], axis=1)
        swapped = mm(blocks, swap).astype(BF16)
        for half in range(2):
            attsend[((pair % 2) * 2 + half) * 4 + pair // 2] = swapped[:, half * ROWS:(half + 1) * ROWS]
    each(1, N_SEQ, lambda i: a_copy(i, sq).start())
    self_att = pltpu.make_async_copy(attsend.at[u * 4 + v], attin.at[sq], local.at[5])
    self_att.start()

    each(0, 4, lambda i: p_forward(i, 1 - core).wait_recv())
    for pair in range(N_SEQ // 2):
        rows = pl.ds(pair * 2 * HD, 2 * HD)
        row, col = pair // 2, (pair % 2) * 2
        left = jnp.concatenate([pwall[0, row, col].astype(F32), pwall[0, row, col + 1].astype(F32)], axis=0)
        right = jnp.concatenate([pwall[1, col, row].astype(F32), pwall[1, col + 1, row].astype(F32)], axis=0)
        pwcat[rows, 0:HALF] = left.astype(BF16)
        pwcat[rows, HALF:D] = right[:, HALF - REST:].astype(BF16)

    self_att.wait()
    each(1, N_SEQ, lambda i: a_copy(i, (sq - i + N_SEQ) % N_SEQ).wait_recv())
    heads = attin[...].astype(F32).reshape(N_SEQ * HD, ROWS).astype(BF16)
    for part in range(2):
        half_rows = ROWS // 2
        cut = slice(part * half_rows, (part + 1) * half_rows)
        joined = mm_nt(unroute[cut, :], heads).astype(BF16)
        branch = mm(joined, pwcat[...])
        where = clip_col[cut, 0:1]
        clip = where >> 6
        position = ((where >> 2) & 15) * 64 + sq * 4 + (where & 3)
        limit = jnp.where(clip == 0, length[0, 0], jnp.where(
            clip == 1, length[0, 1], jnp.where(clip == 2, length[0, 2], length[0, 3])))
        rows = arrived[part * 16:(part + 1) * 16].astype(F32).reshape(half_rows, D)
        result = jnp.where(position < limit, rows + of_its_clip(clip, 2) * branch, 0.0)
        ret[part * 16:(part + 1) * 16] = result.reshape(16, 8, D).astype(BF16)
        each(part * 16 + 1 - part, part * 16 + 16, lambda i: ret_out(i).start())
    self_back = pltpu.make_async_copy(ret.at[0], back.at[0], local.at[6])
    self_back.start()

    for step in (1, 2, 3):
        w_copy(step, v).wait_send()
        p_first(step, v).wait_send()
        p_second(step, u).wait_send()
        for k in range(CHUNKS):
            hid_copy(k, step, u).wait_send()
            x_copy(k, step, v).wait_send()
    each(1, N_DP, lambda i: tok_out(i).wait_send())
    each(0, 4, lambda i: p_forward(i, core).wait_send())
    each(1, N_SEQ, lambda i: a_copy(i, sq).wait_send())

    self_back.wait()
    each(1, N_DP, lambda i: ret_out(i).wait_recv())
    returned = back[...].astype(F32).reshape(ROWS, D).astype(BF16)
    out[...] = mm(route[...], returned).astype(BF16)
    each(1, N_DP, lambda i: ret_out(i).wait_send())


def body(tokens, slot_owner, clip_pieces, clip_length, modulation, qkv_weight, qk_gain, proj_weight):
    vmem = pl.BlockSpec(memory_space=pltpu.VMEM)
    smem = pl.BlockSpec(memory_space=pltpu.SMEM)
    dma = pltpu.SemaphoreType.DMA
    result = pl.pallas_call(
        kernel,
        out_shape=jax.ShapeDtypeStruct((ROWS, D), BF16),
        in_specs=[vmem, vmem, vmem, smem, vmem, vmem, vmem, vmem],
        out_specs=vmem,
        scratch_shapes=[
            pltpu.VMEM((N_DP, 8, D), BF16),
            pltpu.VMEM((N_DP, 8, D), BF16),
            pltpu.VMEM((CHUNKS, NY, CHUNK_ROWS, D), BF16),
            pltpu.VMEM((NX, 3, HD, D), BF16),
            pltpu.VMEM((NX * 3 * HD, D), BF16),
            pltpu.VMEM((NX * 3 * HD, ROWS), F32),
            pltpu.VMEM((2, 4, 4, HD, HALF), BF16),
            pltpu.VMEM((N_SEQ * HD, D), BF16),
            pltpu.VMEM((CHUNKS, NX, 3, HD, ROWS), BF16),
            pltpu.VMEM((NX, CHUNKS, 3, HD, ROWS), BF16),
            pltpu.VMEM((CLIPS, 8, HD, 128), BF16),
            pltpu.VMEM((CLIPS, 8, 128, HD), BF16),
            pltpu.VMEM((CLIPS, 8, HD + 8, 128), BF16),
            pltpu.VMEM((CLIPS, 8, HD, 128), BF16),
            pltpu.VMEM((N_SEQ, HD, ROWS), BF16),
            pltpu.VMEM((N_SEQ, HD, ROWS), BF16),
            pltpu.VMEM((N_DP, 8, D), BF16),
            pltpu.VMEM((N_DP, 8, D), BF16),
            pltpu.VMEM((512, 512), BF16),
            pltpu.VMEM((512, 512), BF16),
            pltpu.VMEM((ROWS, ROWS), BF16),
            pltpu.VMEM((ROWS, ROWS), BF16),
            pltpu.VMEM((ROWS, 128), I32),
            dma((N_DP,)), dma((N_DP,)),
            dma((CHUNKS, 4)), dma((CHUNKS, 4)), dma((CHUNKS, 4)), dma((CHUNKS, 4)),
            dma((4,)), dma((4,)),
            dma((2, 4)), dma((2, 4)), dma((4,)), dma((4,)), dma((N_SEQ,)), dma((N_SEQ,)),
            dma((N_DP,)), dma((N_DP,)),
            dma((8,)), dma((CHUNKS,)),
        ],
        compiler_params=pltpu.CompilerParams(
            collective_id=0, has_side_effects=True, vmem_limit_bytes=50 * 1024 * 1024
        ),
        cost_estimate=pl.CostEstimate(flops=5 * 10**9, bytes_accessed=4 * 10**6, transcendentals=4 * 10**6),
        name="block",
    )(
        tokens[0].reshape(ROWS, D),
        slot_owner,
        clip_pieces[0],
        clip_length,
        modulation[0].transpose(1, 0, 2),
        qkv_weight.transpose(1, 2, 0),
        qk_gain,
        proj_weight,
    )
    return result.reshape(1, 64, 4, D)


def solution(mesh):
    return jax.shard_map(
        body,
        mesh=mesh,
        in_specs=(
            P("dp", None, "seq", None),
            P("dp", None),
            P("dp", None, None),
            P("dp", None),
            P("dp", None, None, None),
            P(None, None, "seq"),
            P(),
            P("seq", None),
        ),
        out_specs=P("dp", None, "seq", None),
        check_vma=False,
    )
```

```python
import math

import jax
import jax.numpy as jnp
from jax import lax
from jax.experimental import pallas as pl
from jax.experimental.pallas import tpu as pltpu
from jax.sharding import PartitionSpec as P

MESH = pl.DeviceIdType.MESH
F32 = jnp.float32
BF16 = jnp.bfloat16
I32 = jnp.int32
D = 1152
HD = 72
N_DP = 32
N_SEQ = 16
NX = 4
NY = 4
CLIPS = 4
HALF = 640
REST = D - HALF
CHUNKS = 4
PER_CHUNK = N_DP // CHUNKS
ROWS = 256
CHUNK_ROWS = ROWS // CHUNKS
EPSILON = 1e-06


def iota(shape, dim):
    return lax.broadcasted_iota(I32, shape, dim)


def mm(a, b):
    return lax.dot_general(a, b, (((1,), (0,)), ((), ())), preferred_element_type=F32)


def mm_nt(a, b):
    return lax.dot_general(a, b, (((1,), (1,)), ((), ())), preferred_element_type=F32)


def out_slot(distance, owner_core):
    return owner_core * 16 + (distance & 3) * 4 + (distance >> 2)


def in_slot(distance, source_core):
    return (distance & 3) * PER_CHUNK + (distance >> 2) * 2 + source_core


def column_of(row, n):
    spread = jnp.broadcast_to(row.astype(F32), (n, n))
    picked = jnp.where(iota((n, n), 0) == iota((n, n), 1), spread, 0.0)
    return jnp.sum(picked, axis=1, keepdims=True).astype(I32)


def kernel(
    tok, owner, table, length, mod, w, gain, pw, out,
    outgoing, arrived, hid, wall, wcat, res, pwall, pwcat, stage, qkv, qc, kc, vc, att, attsend, attin,
    ret, back, spread, spread_t, unroute, route, clip_col,
    dp_send, dp_recv, y_send, y_recv, x_send, x_recv, w_send, w_recv, wf_send, wf_recv,
    p_send, p_recv, pf_send, pf_recv, a_send, a_recv, r_send, r_recv, local, x_local,
):
    me = lax.axis_index("dp")
    sq = lax.axis_index("seq")
    core = me % 2
    sibling = me + 1 - 2 * core
    z = me // 2
    u = sq // NX
    v = sq % NX
    pu = v * (1 - core) + u * core
    pv = u * (1 - core) + v * core

    def seq_at(u_of, v_of):
        return u_of * NX + v_of

    def p_at(u_of, v_of):
        return (v_of * NX + u_of) * (1 - core) + (u_of * NX + v_of) * core

    def ahead(position, step):
        return (position + step) % 4

    def behind(position, step):
        return (position - step + 4) % 4

    def remote(src, dst, send, recv, dp, seq):
        return pltpu.make_async_remote_copy(
            src_ref=src, dst_ref=dst, send_sem=send, recv_sem=recv,
            device_id={"dp": dp, "seq": seq}, device_id_type=MESH,
        )

    def tok_out(i):
        rank = i % 16
        distance = (rank % 4) * 4 + rank // 4
        to = (distance % 4) * PER_CHUNK + (distance // 4) * 2 + core
        return remote(
            outgoing.at[i], arrived.at[to], dp_send.at[i], dp_recv.at[to], ((z + distance) % 16) * 2 + i // 16, sq
        )

    def tok_in(slot):
        return remote(outgoing.at[slot], arrived.at[slot], dp_send.at[slot], dp_recv.at[slot], sibling, sq)

    def ret_out(slot):
        distance = slot // PER_CHUNK + ((slot % PER_CHUNK) // 2) * 4
        to = core * 16 + (distance % 4) * 4 + distance // 4
        return remote(
            ret.at[slot], back.at[to], r_send.at[slot], r_recv.at[to], ((z - distance + 16) % 16) * 2 + slot % 2, sq
        )

    def ret_in(slot):
        return remote(ret.at[slot], back.at[slot], r_send.at[slot], r_recv.at[slot], sibling, sq)

    def hid_copy(k, step, row):
        return remote(
            hid.at[k, row], hid.at[k, row], y_send.at[k, step], y_recv.at[k, step], me, seq_at(ahead(u, step), v)
        )

    def w_copy(step, col):
        return remote(wall.at[col], wall.at[col], w_send.at[step], w_recv.at[step], me, seq_at(u, ahead(v, step)))

    def w_forward(step):
        col = behind(v, step)
        return remote(wall.at[col], wall.at[col], wf_send.at[step], wf_recv.at[step], sibling, sq)

    def x_copy(k, step, col):
        return remote(
            stage.at[k, ahead(v, step)], qkv.at[col, k], x_send.at[k, step], x_recv.at[k, step],
            me, seq_at(u, ahead(v, step)),
        )

    def p_first(step, col):
        return remote(
            pwall.at[core, pu, col], pwall.at[core, pu, col], p_send.at[0, step], p_recv.at[0, step],
            me, p_at(pu, ahead(pv, step)),
        )

    def p_second(step, row):
        return remote(
            pwall.at[core, row], pwall.at[core, row], p_send.at[1, step], p_recv.at[1, step],
            me, p_at(ahead(pu, step), pv),
        )

    def p_forward(row, half):
        return remote(pwall.at[half, row], pwall.at[half, row], pf_send.at[row], pf_recv.at[row], sibling, sq)

    def a_copy(step, head):
        to = (sq + step) % N_SEQ
        return remote(attsend.at[to], attin.at[head], a_send.at[step], a_recv.at[step], me, to)

    def each(first, last, action):
        lax.fori_loop(first, last, lambda i, c: (action(i), c)[1], 0)

    def on_core(which, *actions):
        @pl.when(core == which)
        def _():
            for action in actions:
                action()

    barrier = pltpu.get_barrier_semaphore()
    each(1, N_DP, lambda i: pl.semaphore_signal(
        barrier, inc=1, device_id={"dp": (me + i) % N_DP, "seq": sq}, device_id_type=MESH))
    each(1, N_SEQ, lambda i: pl.semaphore_signal(
        barrier, inc=1, device_id={"dp": me, "seq": (sq + i) % N_SEQ}, device_id_type=MESH))

    cols = pl.ds(pl.multiple_of(core * REST, 128), HALF)
    own_w = pltpu.make_async_copy(w, wall.at[v], local.at[0])
    own_p = pltpu.make_async_copy(pw.at[:, cols], pwall.at[core, pu, pv], local.at[1])
    own_w.start()
    own_p.start()

    owners = owner[...]
    owners_f = jnp.broadcast_to(owners.astype(F32), (64, 64))
    owners_col = column_of(owners, 64).astype(F32)
    earlier = (owners_col == owners_f) & (iota((64, 64), 0) < iota((64, 64), 1))
    rank = jnp.sum(jnp.where(earlier, 1.0, 0.0), axis=0, keepdims=True).astype(I32)
    piece_key = out_slot(((owners >> 1) - z + 16) & 15, owners & 1) * 8 + rank * 4
    widen = jnp.where((iota((64, ROWS), 1) >> 2) == iota((64, ROWS), 0), 1.0, 0.0).astype(BF16)
    keys = mm(jnp.broadcast_to(piece_key.astype(F32), (16, 64)).astype(BF16), widen)[0:1].astype(I32)
    keys = keys + (iota((1, ROWS), 1) & 3)
    route_rows = jnp.where(iota((ROWS, ROWS), 0) == keys, 1.0, 0.0).astype(BF16)
    outgoing[...] = mm(route_rows, tok[...]).reshape(N_DP, 8, D).astype(BF16)

    pl.semaphore_wait(barrier, N_DP - 1 + N_SEQ - 1)

    own_w.wait()
    own_p.wait()
    self_in = pltpu.make_async_copy(outgoing.at[core * 16], arrived.at[core], local.at[4])
    self_in.start()
    to_sibling = tok_out((1 - core) * 16)

    each(1, 16, lambda i: tok_out(i).start())
    to_sibling.start()
    for step in (2, 1, 3):
        p_first(step, pv).start()
    on_core(0, lambda: [w_copy(step, v).start() for step in (2, 1, 3)])

    keys_col = column_of(keys, ROWS)
    route[...] = jnp.where(iota((ROWS, ROWS), 1) == keys_col, 1.0, 0.0).astype(BF16)

    def arrival_row(pieces, row):
        source, rank_of = pieces >> 1, pieces & 1
        return in_slot((z - (source >> 1) + 16) & 15, source & 1) * 8 + rank_of * 4 + row

    def table_row(width, clip_shift):
        lane = iota((16, width), 1)
        pick = jnp.where(((lane >> 2) & 15) == iota((16, width), 0), 1.0, 0.0).astype(BF16)
        wide = mm(table[...].astype(F32).astype(BF16), pick)
        mine = (iota((CLIPS, width), 1) >> clip_shift) == iota((CLIPS, width), 0)
        pieces = jnp.sum(jnp.where(mine, wide, 0.0), axis=0, keepdims=True).astype(I32)
        return arrival_row(pieces, iota((1, width), 1) & 3)

    key_short = table_row(ROWS, 6)
    of_clip = iota((ROWS, ROWS), 0) == key_short
    unroute[...] = jnp.where(of_clip, 1.0, 0.0).astype(BF16)
    place = jnp.sum(jnp.where(of_clip, iota((ROWS, ROWS), 1).astype(F32), 0.0), axis=1, keepdims=True)
    clip_col[...] = jnp.broadcast_to(place.astype(I32), (ROWS, 128))
    key_long = table_row(2 * ROWS, 7)
    wide_lane = iota((1, 2 * ROWS), 1)
    key_long = (key_long >> 6) * 128 + ((wide_lane >> 6) & 1) * 64 + (key_long & 63)
    spread[...] = jnp.where(iota((512, 512), 0) == key_long, 1.0, 0.0).astype(BF16)
    spread_t[...] = jnp.where(iota((512, 512), 1) == column_of(key_long, 512), 1.0, 0.0).astype(BF16)

    def of_its_clip(clip, which):
        factors = mod[which].astype(F32)
        rows = [factors[c:c + 1, :] for c in range(CLIPS)]
        return jnp.where(clip == 0, rows[0], jnp.where(clip == 1, rows[1], jnp.where(clip == 2, rows[2], rows[3])))

    def chunk_in(k):
        if k == 0:
            self_in.wait()
            tok_in(1 - core).wait_recv()
        each(k * PER_CHUNK + (2 if k == 0 else 0), (k + 1) * PER_CHUNK, lambda i: tok_in(i).wait_recv())
        rows = arrived[pl.ds(k * PER_CHUNK, PER_CHUNK)].astype(F32).reshape(CHUNK_ROWS, D)
        clip = clip_col[pl.ds(pl.multiple_of(k * CHUNK_ROWS, CHUNK_ROWS), CHUNK_ROWS), 0:1] >> 6
        centered = rows - jnp.mean(rows, axis=-1, keepdims=True)
        variance = jnp.mean(centered * centered, axis=-1, keepdims=True)
        normed = centered * lax.rsqrt(variance + EPSILON)
        hidden = normed * (1.0 + of_its_clip(clip, 1)) + of_its_clip(clip, 0)
        hid[k, pl.ds(u, 1)] = hidden.astype(BF16)[None]
        for step in (2, 1, 3):
            hid_copy(k, step, u).start()

    gains = []
    for i in range(2):
        spread_gain = jnp.broadcast_to(gain[i:i + 1, :], (HD, HD))
        picked = jnp.where(iota((HD, HD), 0) == iota((HD, HD), 1), spread_gain, 0.0)
        gains.append(jnp.sum(picked, axis=1, keepdims=True))

    def own_stage(k):
        return pltpu.make_async_copy(stage.at[k, v], qkv.at[v, k], x_local.at[k])

    def chunk_qkv(k):
        for step in (1, 2, 3):
            hid_copy(k, step, behind(u, step)).wait_recv()
        rows = hid[k].reshape(ROWS, D)
        res[...] = mm_nt(wcat[...], rows)
        for head in range(NX):
            base = head * 3 * HD
            for part in range(2):
                block = res[base + part * HD:base + (part + 1) * HD, :]
                mean_square = jnp.mean(block * block, axis=0, keepdims=True)
                stage[k, head, part] = (block * lax.rsqrt(mean_square + EPSILON) * gains[part]).astype(BF16)
            stage[k, head, 2] = res[base + 2 * HD:base + 3 * HD, :].astype(BF16)
        for step in (2, 1, 3):
            x_copy(k, step, v).start()
        own_stage(k).start()

    def second_batch():
        each(17, N_DP, lambda i: tok_out(i).start())

    def rest_of_projection():
        for step in (1, 2, 3):
            p_first(step, behind(pv, step)).wait_recv()
        for step in (2, 1, 3):
            p_second(step, pu).start()

    def hand_over():
        for step in (1, 2, 3):
            p_second(step, behind(pu, step)).wait_recv()
        each(0, 4, lambda i: p_forward(i, core).start())

    on_core(1, lambda: each(1, 16, lambda i: tok_out(i).wait_send()), second_batch)
    chunk_in(0)
    on_core(0, second_batch)

    def weights_in():
        for step in (1, 2, 3):
            w_copy(step, behind(v, step)).wait_recv()
            w_forward(step).start()

    chunk_in(1)
    on_core(0, weights_in, rest_of_projection)
    chunk_in(2)
    chunk_in(3)
    on_core(1, rest_of_projection)

    on_core(1, lambda: [w_forward(step).wait_recv() for step in (1, 2, 3)])
    for pair in range(2):
        rows = wall[2 * pair:2 * pair + 2].astype(F32).reshape(6 * HD, D)
        wcat[pair * 6 * HD:(pair + 1) * 6 * HD, :] = rows.astype(BF16)
    chunk_qkv(0)
    chunk_qkv(1)
    chunk_qkv(2)
    chunk_qkv(3)
    on_core(0, hand_over)

    for k in range(CHUNKS):
        own_stage(k).wait()
        for step in (1, 2, 3):
            x_copy(k, step, behind(v, step)).wait_recv()
    lane = iota((1, 128), 1)

    def to_clips(col, carry):
        for pair in range(2):
            def part_of(part):
                blocks = [qkv[col, k, part, :, pair * 128:(pair + 1) * 128] for k in range(CHUNKS)]
                return jnp.concatenate(blocks, axis=1)
            queries = mm(part_of(0), spread[...]).astype(BF16)
            keys_of = mm_nt(spread_t[...], part_of(1)).astype(BF16)
            values = mm(part_of(2), spread[...])
            for clip in range(CLIPS):
                cut = slice(clip * 128, (clip + 1) * 128)
                qc[clip, col * 2 + pair] = queries[:, cut]
                kc[clip, col * 2 + pair] = keys_of[cut, :]
                holder = jnp.where(lane < 64, seq_at(pair * 2, col), seq_at(pair * 2 + 1, col))
                position = ((lane >> 2) & 15) * 64 + holder * 4 + (lane & 3)
                inside = jnp.where(position < length[0, clip], 1.0, 0.0)
                ones = jnp.broadcast_to(inside, (8, 128))
                vc[clip, col * 2 + pair] = jnp.concatenate([values[:, cut] * inside, ones], axis=0).astype(BF16)
        return carry

    lax.fori_loop(0, NX, to_clips, 0)
    on_core(1, hand_over)

    factor = math.log2(math.e) / math.sqrt(HD)

    def attend(clip, carry):
        keys_of = kc[clip].reshape(8 * 128, HD)
        values = jnp.concatenate([vc[clip, j] for j in range(8)], axis=1)
        for block in range(4):
            queries = jnp.concatenate([qc[clip, 2 * block], qc[clip, 2 * block + 1]], axis=1)
            scores = mm(keys_of, queries)
            unscaled = jnp.exp2(scores * factor).astype(BF16)
            summed = mm(values, unscaled)
            attended = (summed[0:HD] / summed[HD:HD + 1]).astype(BF16)
            att[clip, 2 * block] = attended[:, 0:128]
            att[clip, 2 * block + 1] = attended[:, 128:256]
        return carry

    lax.fori_loop(0, CLIPS, attend, 0)

    come = iota((512, 512), 0)
    go = iota((512, 512), 1)
    swap = jnp.where(come == ((go >> 6) & 3) * 128 + (go >> 8) * 64 + (go & 63), 1.0, 0.0).astype(BF16)
    for pair in range(8):
        blocks = jnp.concatenate([att[clip, pair] for clip in range(CLIPS)], axis=1)
        swapped = mm(blocks, swap).astype(BF16)
        for half in range(2):
            attsend[((pair % 2) * 2 + half) * 4 + pair // 2] = swapped[:, half * ROWS:(half + 1) * ROWS]
    each(1, N_SEQ, lambda i: a_copy(i, sq).start())
    self_att = pltpu.make_async_copy(attsend.at[sq], attin.at[sq], local.at[5])
    self_att.start()

    each(0, 4, lambda i: p_forward(i, 1 - core).wait_recv())
    for pair in range(N_SEQ // 2):
        rows = pl.ds(pair * 2 * HD, 2 * HD)
        row, col = pair // 2, (pair % 2) * 2
        left = jnp.concatenate([pwall[0, col, row].astype(F32), pwall[0, col + 1, row].astype(F32)], axis=0)
        right = jnp.concatenate([pwall[1, row, col].astype(F32), pwall[1, row, col + 1].astype(F32)], axis=0)
        pwcat[rows, 0:HALF] = left.astype(BF16)
        pwcat[rows, HALF:D] = right[:, HALF - REST:].astype(BF16)

    self_att.wait()
    each(1, N_SEQ, lambda i: a_copy(i, (sq - i + N_SEQ) % N_SEQ).wait_recv())
    heads = attin[...].astype(F32).reshape(N_SEQ * HD, ROWS).astype(BF16)
    for part in range(2):
        half_rows = ROWS // 2
        cut = slice(part * half_rows, (part + 1) * half_rows)
        joined = mm_nt(unroute[cut, :], heads).astype(BF16)
        branch = mm(joined, pwcat[...])
        where = clip_col[cut, 0:1]
        clip = where >> 6
        position = ((where >> 2) & 15) * 64 + sq * 4 + (where & 3)
        limit = jnp.where(clip == 0, length[0, 0], jnp.where(
            clip == 1, length[0, 1], jnp.where(clip == 2, length[0, 2], length[0, 3])))
        rows = arrived[part * 16:(part + 1) * 16].astype(F32).reshape(half_rows, D)
        result = jnp.where(position < limit, rows + of_its_clip(clip, 2) * branch, 0.0)
        ret[part * 16:(part + 1) * 16] = result.reshape(16, 8, D).astype(BF16)
        each(part * 16 + 2 * (1 - part), part * 16 + 16, lambda i: ret_out(i).start())
    ret_out(1 - core).start()
    self_back = pltpu.make_async_copy(ret.at[core], back.at[core * 16], local.at[6])
    self_back.start()

    for step in (1, 2, 3):
        p_first(step, pv).wait_send()
        p_second(step, pu).wait_send()
        for k in range(CHUNKS):
            hid_copy(k, step, u).wait_send()
            x_copy(k, step, v).wait_send()
    @pl.when(core == 0)
    def _():
        each(1, 16, lambda i: tok_out(i).wait_send())
        for step in (1, 2, 3):
            w_copy(step, v).wait_send()
            w_forward(step).wait_send()

    to_sibling.wait_send()
    each(17, N_DP, lambda i: tok_out(i).wait_send())
    each(0, 4, lambda i: p_forward(i, core).wait_send())
    each(1, N_SEQ, lambda i: a_copy(i, sq).wait_send())

    self_back.wait()
    ret_in((1 - core) * 16).wait_recv()
    each(1, 16, lambda i: ret_in(i).wait_recv())
    each(17, N_DP, lambda i: ret_in(i).wait_recv())
    returned = back[...].astype(F32).reshape(ROWS, D).astype(BF16)
    out[...] = mm(route[...], returned).astype(BF16)
    ret_out(1 - core).wait_send()
    each(2, N_DP, lambda i: ret_out(i).wait_send())


def body(tokens, slot_owner, clip_pieces, clip_length, modulation, qkv_weight, qk_gain, proj_weight):
    vmem = pl.BlockSpec(memory_space=pltpu.VMEM)
    smem = pl.BlockSpec(memory_space=pltpu.SMEM)
    dma = pltpu.SemaphoreType.DMA
    result = pl.pallas_call(
        kernel,
        out_shape=jax.ShapeDtypeStruct((ROWS, D), BF16),
        in_specs=[vmem, vmem, vmem, smem, vmem, vmem, vmem, vmem],
        out_specs=vmem,
        scratch_shapes=[
            pltpu.VMEM((N_DP, 8, D), BF16),
            pltpu.VMEM((N_DP, 8, D), BF16),
            pltpu.VMEM((CHUNKS, NY, CHUNK_ROWS, D), BF16),
            pltpu.VMEM((NX, 3, HD, D), BF16),
            pltpu.VMEM((NX * 3 * HD, D), BF16),
            pltpu.VMEM((NX * 3 * HD, ROWS), F32),
            pltpu.VMEM((2, 4, 4, HD, HALF), BF16),
            pltpu.VMEM((N_SEQ * HD, D), BF16),
            pltpu.VMEM((CHUNKS, NX, 3, HD, ROWS), BF16),
            pltpu.VMEM((NX, CHUNKS, 3, HD, ROWS), BF16),
            pltpu.VMEM((CLIPS, 8, HD, 128), BF16),
            pltpu.VMEM((CLIPS, 8, 128, HD), BF16),
            pltpu.VMEM((CLIPS, 8, HD + 8, 128), BF16),
            pltpu.VMEM((CLIPS, 8, HD, 128), BF16),
            pltpu.VMEM((N_SEQ, HD, ROWS), BF16),
            pltpu.VMEM((N_SEQ, HD, ROWS), BF16),
            pltpu.VMEM((N_DP, 8, D), BF16),
            pltpu.VMEM((N_DP, 8, D), BF16),
            pltpu.VMEM((512, 512), BF16),
            pltpu.VMEM((512, 512), BF16),
            pltpu.VMEM((ROWS, ROWS), BF16),
            pltpu.VMEM((ROWS, ROWS), BF16),
            pltpu.VMEM((ROWS, 128), I32),
            dma((N_DP,)), dma((N_DP,)),
            dma((CHUNKS, 4)), dma((CHUNKS, 4)), dma((CHUNKS, 4)), dma((CHUNKS, 4)),
            dma((4,)), dma((4,)), dma((4,)), dma((4,)),
            dma((2, 4)), dma((2, 4)), dma((4,)), dma((4,)), dma((N_SEQ,)), dma((N_SEQ,)),
            dma((N_DP,)), dma((N_DP,)),
            dma((8,)), dma((CHUNKS,)),
        ],
        compiler_params=pltpu.CompilerParams(
            collective_id=0, has_side_effects=True, vmem_limit_bytes=50 * 1024 * 1024
        ),
        cost_estimate=pl.CostEstimate(flops=5 * 10**9, bytes_accessed=4 * 10**6, transcendentals=4 * 10**6),
        name="block",
    )(
        tokens[0].reshape(ROWS, D),
        slot_owner,
        clip_pieces[0],
        clip_length,
        modulation[0].transpose(1, 0, 2),
        qkv_weight.transpose(1, 2, 0),
        qk_gain,
        proj_weight,
    )
    return result.reshape(1, 64, 4, D)


def solution(mesh):
    return jax.shard_map(
        body,
        mesh=mesh,
        in_specs=(
            P("dp", None, "seq", None),
            P("dp", None),
            P("dp", None, None),
            P("dp", None),
            P("dp", None, None, None),
            P(None, None, "seq"),
            P(),
            P("seq", None),
        ),
        out_specs=P("dp", None, "seq", None),
        check_vma=False,
    )
```

```python
import math

import jax
import jax.numpy as jnp
from jax import lax
from jax.experimental import pallas as pl
from jax.experimental.pallas import tpu as pltpu
from jax.sharding import PartitionSpec as P

MESH = pl.DeviceIdType.MESH
F32 = jnp.float32
BF16 = jnp.bfloat16
I32 = jnp.int32
D = 1152
HD = 72
N_DP = 32
N_SEQ = 16
NX = 4
NY = 4
CLIPS = 4
HALF = 640
REST = D - HALF
CHUNKS = 4
PER_CHUNK = N_DP // CHUNKS
ROWS = 256
CHUNK_ROWS = ROWS // CHUNKS
EPSILON = 1e-06


def iota(shape, dim):
    return lax.broadcasted_iota(I32, shape, dim)


def mm(a, b):
    return lax.dot_general(a, b, (((1,), (0,)), ((), ())), preferred_element_type=F32)


def mm_nt(a, b):
    return lax.dot_general(a, b, (((1,), (1,)), ((), ())), preferred_element_type=F32)


def out_slot(distance, owner_core):
    return owner_core * 16 + (distance & 3) * 4 + (distance >> 2)


def in_slot(distance, source_core):
    return (distance & 3) * PER_CHUNK + (distance >> 2) * 2 + source_core


def column_of(row, n):
    spread = jnp.broadcast_to(row.astype(F32), (n, n))
    picked = jnp.where(iota((n, n), 0) == iota((n, n), 1), spread, 0.0)
    return jnp.sum(picked, axis=1, keepdims=True).astype(I32)


def kernel(
    tok, owner, table, length, mod, w, gain, pw, out,
    outgoing, arrived, hid, wall, wcat, res, pwall, pwcat, stage, qkv, qc, kc, vc, att, attsend, attin,
    ret, back, spread, spread_t, unroute, route, clip_col,
    dp_send, dp_recv, y_send, y_recv, x_send, x_recv, w_send, w_recv, wf_send, wf_recv,
    p_send, p_recv, pf_send, pf_recv, a_send, a_recv, r_send, r_recv, local, x_local,
):
    me = lax.axis_index("dp")
    sq = lax.axis_index("seq")
    core = me % 2
    sibling = me + 1 - 2 * core
    z = me // 2
    u = sq // NX
    v = sq % NX
    pu = v * (1 - core) + u * core
    pv = u * (1 - core) + v * core

    def seq_at(u_of, v_of):
        return u_of * NX + v_of

    def p_at(u_of, v_of):
        return (v_of * NX + u_of) * (1 - core) + (u_of * NX + v_of) * core

    def ahead(position, step):
        return (position + step) % 4

    def behind(position, step):
        return (position - step + 4) % 4

    def remote(src, dst, send, recv, dp, seq):
        return pltpu.make_async_remote_copy(
            src_ref=src, dst_ref=dst, send_sem=send, recv_sem=recv,
            device_id={"dp": dp, "seq": seq}, device_id_type=MESH,
        )

    def tok_out(i):
        rank = i % 16
        distance = (rank % 4) * 4 + rank // 4
        to = (distance % 4) * PER_CHUNK + (distance // 4) * 2 + core
        return remote(
            outgoing.at[i], arrived.at[to], dp_send.at[i], dp_recv.at[to], ((z + distance) % 16) * 2 + i // 16, sq
        )

    def tok_in(slot):
        return remote(outgoing.at[slot], arrived.at[slot], dp_send.at[slot], dp_recv.at[slot], sibling, sq)

    def ret_out(slot):
        distance = slot // PER_CHUNK + ((slot % PER_CHUNK) // 2) * 4
        to = core * 16 + (distance % 4) * 4 + distance // 4
        return remote(
            ret.at[slot], back.at[to], r_send.at[slot], r_recv.at[to], ((z - distance + 16) % 16) * 2 + slot % 2, sq
        )

    def ret_in(slot):
        return remote(ret.at[slot], back.at[slot], r_send.at[slot], r_recv.at[slot], sibling, sq)

    def hid_copy(k, step, row):
        return remote(
            hid.at[k, row], hid.at[k, row], y_send.at[k, step], y_recv.at[k, step], me, seq_at(ahead(u, step), v)
        )

    def w_copy(step, col):
        return remote(wall.at[col], wall.at[col], w_send.at[step], w_recv.at[step], me, seq_at(u, ahead(v, step)))

    def w_forward(step):
        col = behind(v, step)
        return remote(wall.at[col], wall.at[col], wf_send.at[step], wf_recv.at[step], sibling, sq)

    def x_copy(k, step, col):
        return remote(
            stage.at[k, ahead(v, step)], qkv.at[col, k], x_send.at[k, step], x_recv.at[k, step],
            me, seq_at(u, ahead(v, step)),
        )

    def p_first(step, col):
        return remote(
            pwall.at[core, pu, col], pwall.at[core, pu, col], p_send.at[0, step], p_recv.at[0, step],
            me, p_at(pu, ahead(pv, step)),
        )

    def p_second(step, row):
        return remote(
            pwall.at[core, row], pwall.at[core, row], p_send.at[1, step], p_recv.at[1, step],
            me, p_at(ahead(pu, step), pv),
        )

    def p_forward(row, half):
        return remote(pwall.at[half, row], pwall.at[half, row], pf_send.at[row], pf_recv.at[row], sibling, sq)

    def a_copy(h, step, head):
        to = (sq + step) % N_SEQ
        return remote(attsend.at[h, to], attin.at[h, head], a_send.at[h, step], a_recv.at[h, step], me, to)

    def each(first, last, action):
        lax.fori_loop(first, last, lambda i, c: (action(i), c)[1], 0)

    def on_core(which, *actions):
        @pl.when(core == which)
        def _():
            for action in actions:
                action()

    barrier = pltpu.get_barrier_semaphore()
    each(1, N_DP, lambda i: pl.semaphore_signal(
        barrier, inc=1, device_id={"dp": (me + i) % N_DP, "seq": sq}, device_id_type=MESH))
    each(1, N_SEQ, lambda i: pl.semaphore_signal(
        barrier, inc=1, device_id={"dp": me, "seq": (sq + i) % N_SEQ}, device_id_type=MESH))

    cols = pl.ds(pl.multiple_of(core * REST, 128), HALF)
    own_w = pltpu.make_async_copy(w, wall.at[v], local.at[0])
    own_p = pltpu.make_async_copy(pw.at[:, cols], pwall.at[core, pu, pv], local.at[1])
    own_w.start()
    own_p.start()

    owners = owner[...]
    owners_f = jnp.broadcast_to(owners.astype(F32), (64, 64))
    owners_col = column_of(owners, 64).astype(F32)
    earlier = (owners_col == owners_f) & (iota((64, 64), 0) < iota((64, 64), 1))
    rank = jnp.sum(jnp.where(earlier, 1.0, 0.0), axis=0, keepdims=True).astype(I32)
    piece_key = out_slot(((owners >> 1) - z + 16) & 15, owners & 1) * 8 + rank * 4
    widen = jnp.where((iota((64, ROWS), 1) >> 2) == iota((64, ROWS), 0), 1.0, 0.0).astype(BF16)
    keys = mm(jnp.broadcast_to(piece_key.astype(F32), (16, 64)).astype(BF16), widen)[0:1].astype(I32)
    keys = keys + (iota((1, ROWS), 1) & 3)
    route_rows = jnp.where(iota((ROWS, ROWS), 0) == keys, 1.0, 0.0).astype(BF16)
    outgoing[...] = mm(route_rows, tok[...]).reshape(N_DP, 8, D).astype(BF16)

    pl.semaphore_wait(barrier, N_DP - 1 + N_SEQ - 1)

    own_w.wait()
    own_p.wait()
    self_in = pltpu.make_async_copy(outgoing.at[core * 16], arrived.at[core], local.at[4])
    self_in.start()
    to_sibling = tok_out((1 - core) * 16)

    each(1, 16, lambda i: tok_out(i).start())
    to_sibling.start()
    for step in (2, 1, 3):
        p_first(step, pv).start()
    on_core(0, lambda: [w_copy(step, v).start() for step in (2, 1, 3)])

    keys_col = column_of(keys, ROWS)
    route[...] = jnp.where(iota((ROWS, ROWS), 1) == keys_col, 1.0, 0.0).astype(BF16)

    def arrival_row(pieces, row):
        source, rank_of = pieces >> 1, pieces & 1
        return in_slot((z - (source >> 1) + 16) & 15, source & 1) * 8 + rank_of * 4 + row

    def table_row(width, clip_shift):
        lane = iota((16, width), 1)
        pick = jnp.where(((lane >> 2) & 15) == iota((16, width), 0), 1.0, 0.0).astype(BF16)
        wide = mm(table[...].astype(F32).astype(BF16), pick)
        mine = (iota((CLIPS, width), 1) >> clip_shift) == iota((CLIPS, width), 0)
        pieces = jnp.sum(jnp.where(mine, wide, 0.0), axis=0, keepdims=True).astype(I32)
        return arrival_row(pieces, iota((1, width), 1) & 3)

    key_short = table_row(ROWS, 6)
    of_clip = iota((ROWS, ROWS), 0) == key_short
    unroute[...] = jnp.where(of_clip, 1.0, 0.0).astype(BF16)
    place = jnp.sum(jnp.where(of_clip, iota((ROWS, ROWS), 1).astype(F32), 0.0), axis=1, keepdims=True)
    clip_col[...] = jnp.broadcast_to(place.astype(I32), (ROWS, 128))
    key_long = table_row(2 * ROWS, 7)
    wide_lane = iota((1, 2 * ROWS), 1)
    key_long = (key_long >> 6) * 128 + ((wide_lane >> 6) & 1) * 64 + (key_long & 63)
    spread[...] = jnp.where(iota((512, 512), 0) == key_long, 1.0, 0.0).astype(BF16)
    spread_t[...] = jnp.where(iota((512, 512), 1) == column_of(key_long, 512), 1.0, 0.0).astype(BF16)

    def of_its_clip(clip, which):
        factors = mod[which].astype(F32)
        rows = [factors[c:c + 1, :] for c in range(CLIPS)]
        return jnp.where(clip == 0, rows[0], jnp.where(clip == 1, rows[1], jnp.where(clip == 2, rows[2], rows[3])))

    def chunk_in(k):
        if k == 0:
            self_in.wait()
            tok_in(1 - core).wait_recv()
        each(k * PER_CHUNK + (2 if k == 0 else 0), (k + 1) * PER_CHUNK, lambda i: tok_in(i).wait_recv())
        rows = arrived[pl.ds(k * PER_CHUNK, PER_CHUNK)].astype(F32).reshape(CHUNK_ROWS, D)
        clip = clip_col[pl.ds(pl.multiple_of(k * CHUNK_ROWS, CHUNK_ROWS), CHUNK_ROWS), 0:1] >> 6
        centered = rows - jnp.mean(rows, axis=-1, keepdims=True)
        variance = jnp.mean(centered * centered, axis=-1, keepdims=True)
        normed = centered * lax.rsqrt(variance + EPSILON)
        hidden = normed * (1.0 + of_its_clip(clip, 1)) + of_its_clip(clip, 0)
        hid[k, pl.ds(u, 1)] = hidden.astype(BF16)[None]
        for step in (2, 1, 3):
            hid_copy(k, step, u).start()

    gains = []
    for i in range(2):
        spread_gain = jnp.broadcast_to(gain[i:i + 1, :], (HD, HD))
        picked = jnp.where(iota((HD, HD), 0) == iota((HD, HD), 1), spread_gain, 0.0)
        gains.append(jnp.sum(picked, axis=1, keepdims=True))

    def own_stage(k):
        return pltpu.make_async_copy(stage.at[k, v], qkv.at[v, k], x_local.at[k])

    def chunk_qkv(k):
        for step in (1, 2, 3):
            hid_copy(k, step, behind(u, step)).wait_recv()
        rows = hid[k].reshape(ROWS, D)
        res[...] = mm_nt(wcat[...], rows)
        for head in range(NX):
            base = head * 3 * HD
            for part in range(2):
                block = res[base + part * HD:base + (part + 1) * HD, :]
                mean_square = jnp.mean(block * block, axis=0, keepdims=True)
                stage[k, head, part] = (block * lax.rsqrt(mean_square + EPSILON) * gains[part]).astype(BF16)
            stage[k, head, 2] = res[base + 2 * HD:base + 3 * HD, :].astype(BF16)
        for step in (2, 1, 3):
            x_copy(k, step, v).start()
        own_stage(k).start()

    def second_batch():
        each(17, N_DP, lambda i: tok_out(i).start())

    def rest_of_projection():
        for step in (1, 2, 3):
            p_first(step, behind(pv, step)).wait_recv()
        for step in (2, 1, 3):
            p_second(step, pu).start()

    def hand_over():
        for step in (1, 2, 3):
            p_second(step, behind(pu, step)).wait_recv()
        each(0, 4, lambda i: p_forward(i, core).start())

    on_core(1, lambda: each(1, 16, lambda i: tok_out(i).wait_send()), second_batch)
    chunk_in(0)
    on_core(0, second_batch)

    def weights_in():
        for step in (1, 2, 3):
            w_copy(step, behind(v, step)).wait_recv()
            w_forward(step).start()

    chunk_in(1)
    on_core(0, weights_in, rest_of_projection)
    chunk_in(2)
    chunk_in(3)
    on_core(1, rest_of_projection)

    on_core(1, lambda: [w_forward(step).wait_recv() for step in (1, 2, 3)])
    for pair in range(2):
        rows = wall[2 * pair:2 * pair + 2].astype(F32).reshape(6 * HD, D)
        wcat[pair * 6 * HD:(pair + 1) * 6 * HD, :] = rows.astype(BF16)
    chunk_qkv(0)
    chunk_qkv(1)
    chunk_qkv(2)
    chunk_qkv(3)
    on_core(0, hand_over)

    for k in range(CHUNKS):
        own_stage(k).wait()
        for step in (1, 2, 3):
            x_copy(k, step, behind(v, step)).wait_recv()
    lane = iota((1, 128), 1)

    def to_clips(col, carry):
        for pair in range(2):
            def part_of(part):
                blocks = [qkv[col, k, part, :, pair * 128:(pair + 1) * 128] for k in range(CHUNKS)]
                return jnp.concatenate(blocks, axis=1)
            queries = mm(part_of(0), spread[...]).astype(BF16)
            keys_of = mm_nt(spread_t[...], part_of(1)).astype(BF16)
            values = mm(part_of(2), spread[...])
            for clip in range(CLIPS):
                cut = slice(clip * 128, (clip + 1) * 128)
                qc[clip, col * 2 + pair] = queries[:, cut]
                kc[clip, col * 2 + pair] = keys_of[cut, :]
                holder = jnp.where(lane < 64, seq_at(pair * 2, col), seq_at(pair * 2 + 1, col))
                position = ((lane >> 2) & 15) * 64 + holder * 4 + (lane & 3)
                inside = jnp.where(position < length[0, clip], 1.0, 0.0)
                ones = jnp.broadcast_to(inside, (8, 128))
                vc[clip, col * 2 + pair] = jnp.concatenate([values[:, cut] * inside, ones], axis=0).astype(BF16)
        return carry

    on_core(1, hand_over)
    lax.fori_loop(0, NX, to_clips, 0)

    factor = math.log2(math.e) / math.sqrt(HD)

    def attend(clip, carry):
        keys_of = kc[clip].reshape(8 * 128, HD)
        values = jnp.concatenate([vc[clip, j] for j in range(8)], axis=1)
        for block in range(4):
            queries = jnp.concatenate([qc[clip, 2 * block], qc[clip, 2 * block + 1]], axis=1)
            scores = mm(keys_of, queries)
            unscaled = jnp.exp2(scores * factor).astype(BF16)
            summed = mm(values, unscaled)
            attended = (summed[0:HD] / summed[HD:HD + 1]).astype(BF16)
            att[clip, 2 * block] = attended[:, 0:128]
            att[clip, 2 * block + 1] = attended[:, 128:256]
        return carry


    come = iota((256, 256), 0)
    go = iota((256, 256), 1)
    swap = jnp.where(come == ((go >> 6) & 1) * 128 + (go >> 7) * 64 + (go & 63), 1.0, 0.0).astype(BF16)

    def self_att(h):
        return pltpu.make_async_copy(attsend.at[h, sq], attin.at[h, sq], local.at[2 + h])

    for h in range(2):
        lax.fori_loop(2 * h, 2 * h + 2, attend, 0)
        for pair in range(8):
            blocks = jnp.concatenate([att[2 * h, pair], att[2 * h + 1, pair]], axis=1)
            swapped = mm(blocks, swap).astype(BF16)
            for half in range(2):
                attsend[h, ((pair % 2) * 2 + half) * 4 + pair // 2] = swapped[:, half * 128:(half + 1) * 128]
        each(1, N_SEQ, lambda i: a_copy(h, i, sq).start())
        self_att(h).start()

    each(0, 4, lambda i: p_forward(i, 1 - core).wait_recv())
    for pair in range(N_SEQ // 2):
        rows = pl.ds(pair * 2 * HD, 2 * HD)
        row, col = pair // 2, (pair % 2) * 2
        left = jnp.concatenate([pwall[0, col, row].astype(F32), pwall[0, col + 1, row].astype(F32)], axis=0)
        right = jnp.concatenate([pwall[1, row, col].astype(F32), pwall[1, row, col + 1].astype(F32)], axis=0)
        pwcat[rows, 0:HALF] = left.astype(BF16)
        pwcat[rows, HALF:D] = right[:, HALF - REST:].astype(BF16)

    for h in range(2):
        self_att(h).wait()
        each(1, N_SEQ, lambda i: a_copy(h, i, (sq - i + N_SEQ) % N_SEQ).wait_recv())
    heads = jnp.concatenate([attin[h].astype(F32).reshape(N_SEQ * HD, 128) for h in range(2)], axis=1).astype(BF16)
    for part in range(2):
        half_rows = ROWS // 2
        cut = slice(part * half_rows, (part + 1) * half_rows)
        joined = mm_nt(unroute[cut, :], heads).astype(BF16)
        branch = mm(joined, pwcat[...])
        where = clip_col[cut, 0:1]
        clip = where >> 6
        position = ((where >> 2) & 15) * 64 + sq * 4 + (where & 3)
        limit = jnp.where(clip == 0, length[0, 0], jnp.where(
            clip == 1, length[0, 1], jnp.where(clip == 2, length[0, 2], length[0, 3])))
        rows = arrived[part * 16:(part + 1) * 16].astype(F32).reshape(half_rows, D)
        result = jnp.where(position < limit, rows + of_its_clip(clip, 2) * branch, 0.0)
        ret[part * 16:(part + 1) * 16] = result.reshape(16, 8, D).astype(BF16)
        each(part * 16 + 2 * (1 - part), part * 16 + 16, lambda i: ret_out(i).start())
    ret_out(1 - core).start()
    self_back = pltpu.make_async_copy(ret.at[core], back.at[core * 16], local.at[6])
    self_back.start()

    for step in (1, 2, 3):
        p_first(step, pv).wait_send()
        p_second(step, pu).wait_send()
        for k in range(CHUNKS):
            hid_copy(k, step, u).wait_send()
            x_copy(k, step, v).wait_send()
    @pl.when(core == 0)
    def _():
        each(1, 16, lambda i: tok_out(i).wait_send())
        for step in (1, 2, 3):
            w_copy(step, v).wait_send()
            w_forward(step).wait_send()

    to_sibling.wait_send()
    each(17, N_DP, lambda i: tok_out(i).wait_send())
    each(0, 4, lambda i: p_forward(i, core).wait_send())
    for h in range(2):
        each(1, N_SEQ, lambda i: a_copy(h, i, sq).wait_send())

    self_back.wait()
    ret_in((1 - core) * 16).wait_recv()
    each(1, 16, lambda i: ret_in(i).wait_recv())
    each(17, N_DP, lambda i: ret_in(i).wait_recv())
    returned = back[...].astype(F32).reshape(ROWS, D).astype(BF16)
    out[...] = mm(route[...], returned).astype(BF16)
    ret_out(1 - core).wait_send()
    each(2, N_DP, lambda i: ret_out(i).wait_send())


def body(tokens, slot_owner, clip_pieces, clip_length, modulation, qkv_weight, qk_gain, proj_weight):
    vmem = pl.BlockSpec(memory_space=pltpu.VMEM)
    smem = pl.BlockSpec(memory_space=pltpu.SMEM)
    dma = pltpu.SemaphoreType.DMA
    result = pl.pallas_call(
        kernel,
        out_shape=jax.ShapeDtypeStruct((ROWS, D), BF16),
        in_specs=[vmem, vmem, vmem, smem, vmem, vmem, vmem, vmem],
        out_specs=vmem,
        scratch_shapes=[
            pltpu.VMEM((N_DP, 8, D), BF16),
            pltpu.VMEM((N_DP, 8, D), BF16),
            pltpu.VMEM((CHUNKS, NY, CHUNK_ROWS, D), BF16),
            pltpu.VMEM((NX, 3, HD, D), BF16),
            pltpu.VMEM((NX * 3 * HD, D), BF16),
            pltpu.VMEM((NX * 3 * HD, ROWS), F32),
            pltpu.VMEM((2, 4, 4, HD, HALF), BF16),
            pltpu.VMEM((N_SEQ * HD, D), BF16),
            pltpu.VMEM((CHUNKS, NX, 3, HD, ROWS), BF16),
            pltpu.VMEM((NX, CHUNKS, 3, HD, ROWS), BF16),
            pltpu.VMEM((CLIPS, 8, HD, 128), BF16),
            pltpu.VMEM((CLIPS, 8, 128, HD), BF16),
            pltpu.VMEM((CLIPS, 8, HD + 8, 128), BF16),
            pltpu.VMEM((CLIPS, 8, HD, 128), BF16),
            pltpu.VMEM((2, N_SEQ, HD, 128), BF16),
            pltpu.VMEM((2, N_SEQ, HD, 128), BF16),
            pltpu.VMEM((N_DP, 8, D), BF16),
            pltpu.VMEM((N_DP, 8, D), BF16),
            pltpu.VMEM((512, 512), BF16),
            pltpu.VMEM((512, 512), BF16),
            pltpu.VMEM((ROWS, ROWS), BF16),
            pltpu.VMEM((ROWS, ROWS), BF16),
            pltpu.VMEM((ROWS, 128), I32),
            dma((N_DP,)), dma((N_DP,)),
            dma((CHUNKS, 4)), dma((CHUNKS, 4)), dma((CHUNKS, 4)), dma((CHUNKS, 4)),
            dma((4,)), dma((4,)), dma((4,)), dma((4,)),
            dma((2, 4)), dma((2, 4)), dma((4,)), dma((4,)), dma((2, N_SEQ)), dma((2, N_SEQ)),
            dma((N_DP,)), dma((N_DP,)),
            dma((8,)), dma((CHUNKS,)),
        ],
        compiler_params=pltpu.CompilerParams(
            collective_id=0, has_side_effects=True, vmem_limit_bytes=50 * 1024 * 1024
        ),
        cost_estimate=pl.CostEstimate(flops=5 * 10**9, bytes_accessed=4 * 10**6, transcendentals=4 * 10**6),
        name="block",
    )(
        tokens[0].reshape(ROWS, D),
        slot_owner,
        clip_pieces[0],
        clip_length,
        modulation[0].transpose(1, 0, 2),
        qkv_weight.transpose(1, 2, 0),
        qk_gain,
        proj_weight,
    )
    return result.reshape(1, 64, 4, D)


def solution(mesh):
    return jax.shard_map(
        body,
        mesh=mesh,
        in_specs=(
            P("dp", None, "seq", None),
            P("dp", None),
            P("dp", None, None),
            P("dp", None),
            P("dp", None, None, None),
            P(None, None, "seq"),
            P(),
            P("seq", None),
        ),
        out_specs=P("dp", None, "seq", None),
        check_vma=False,
    )
```

```python
import math

import jax
import jax.numpy as jnp
from jax import lax
from jax.experimental import pallas as pl
from jax.experimental.pallas import tpu as pltpu
from jax.sharding import PartitionSpec as P

MESH = pl.DeviceIdType.MESH
F32 = jnp.float32
BF16 = jnp.bfloat16
I32 = jnp.int32
D = 1152
HD = 72
N_DP = 32
N_SEQ = 16
NX = 4
NY = 4
CLIPS = 4
HALF = 640
REST = D - HALF
CHUNKS = 4
PER_CHUNK = N_DP // CHUNKS
ROWS = 256
CHUNK_ROWS = ROWS // CHUNKS
EPSILON = 1e-06


def iota(shape, dim):
    return lax.broadcasted_iota(I32, shape, dim)


def mm(a, b):
    return lax.dot_general(a, b, (((1,), (0,)), ((), ())), preferred_element_type=F32)


def mm_nt(a, b):
    return lax.dot_general(a, b, (((1,), (1,)), ((), ())), preferred_element_type=F32)


def out_slot(distance, owner_core):
    return owner_core * 16 + (distance & 3) * 4 + (distance >> 2)


def in_slot(distance, source_core):
    return (distance & 3) * PER_CHUNK + (distance >> 2) * 2 + source_core


def column_of(row, n):
    spread = jnp.broadcast_to(row.astype(F32), (n, n))
    picked = jnp.where(iota((n, n), 0) == iota((n, n), 1), spread, 0.0)
    return jnp.sum(picked, axis=1, keepdims=True).astype(I32)


def kernel(
    tok, owner, table, length, mod, w, gain, pw, out,
    outgoing, arrived, hid, wall, wcat, res, pwall, pwcat, stage, qkv, qc, kc, vc, att, attsend, attin,
    ret, back, spread, spread_t, unroute, route, clip_col,
    dp_send, dp_recv, y_send, y_recv, x_send, x_recv, w_send, w_recv, wf_send, wf_recv,
    p_send, p_recv, pf_send, pf_recv, a_send, a_recv, r_send, r_recv, local, x_local,
):
    me = lax.axis_index("dp")
    sq = lax.axis_index("seq")
    core = me % 2
    sibling = me + 1 - 2 * core
    z = me // 2
    u = sq // NX
    v = sq % NX
    pu = v * (1 - core) + u * core
    pv = u * (1 - core) + v * core

    def seq_at(u_of, v_of):
        return u_of * NX + v_of

    def p_at(u_of, v_of):
        return (v_of * NX + u_of) * (1 - core) + (u_of * NX + v_of) * core

    def ahead(position, step):
        return (position + step) % 4

    def behind(position, step):
        return (position - step + 4) % 4

    def remote(src, dst, send, recv, dp, seq):
        return pltpu.make_async_remote_copy(
            src_ref=src, dst_ref=dst, send_sem=send, recv_sem=recv,
            device_id={"dp": dp, "seq": seq}, device_id_type=MESH,
        )

    def tok_out(i):
        rank = i % 16
        distance = (rank % 4) * 4 + rank // 4
        to = (distance % 4) * PER_CHUNK + (distance // 4) * 2 + core
        return remote(
            outgoing.at[i], arrived.at[to], dp_send.at[i], dp_recv.at[to], ((z + distance) % 16) * 2 + i // 16, sq
        )

    def tok_in(slot):
        return remote(outgoing.at[slot], arrived.at[slot], dp_send.at[slot], dp_recv.at[slot], sibling, sq)

    def ret_out(slot):
        distance = slot // PER_CHUNK + ((slot % PER_CHUNK) // 2) * 4
        to = core * 16 + (distance % 4) * 4 + distance // 4
        return remote(
            ret.at[slot], back.at[to], r_send.at[slot], r_recv.at[to], ((z - distance + 16) % 16) * 2 + slot % 2, sq
        )

    def ret_in(slot):
        return remote(ret.at[slot], back.at[slot], r_send.at[slot], r_recv.at[slot], sibling, sq)

    def hid_copy(k, step, row):
        return remote(
            hid.at[k, row], hid.at[k, row], y_send.at[k, step], y_recv.at[k, step], me, seq_at(ahead(u, step), v)
        )

    def w_copy(step, col):
        return remote(wall.at[col], wall.at[col], w_send.at[step], w_recv.at[step], me, seq_at(u, ahead(v, step)))

    def w_forward(step):
        col = behind(v, step)
        return remote(wall.at[col], wall.at[col], wf_send.at[step], wf_recv.at[step], sibling, sq)

    def x_copy(k, step, col):
        return remote(
            stage.at[k, ahead(v, step)], qkv.at[col, k], x_send.at[k, step], x_recv.at[k, step],
            me, seq_at(u, ahead(v, step)),
        )

    def p_first(step, col):
        return remote(
            pwall.at[core, pu, col], pwall.at[core, pu, col], p_send.at[0, step], p_recv.at[0, step],
            me, p_at(pu, ahead(pv, step)),
        )

    def p_second(step, row):
        return remote(
            pwall.at[core, row], pwall.at[core, row], p_send.at[1, step], p_recv.at[1, step],
            me, p_at(ahead(pu, step), pv),
        )

    def p_forward(row, half):
        return remote(pwall.at[half, row], pwall.at[half, row], pf_send.at[row], pf_recv.at[row], sibling, sq)

    def a_copy(h, step, head):
        to = (sq + step) % N_SEQ
        return remote(attsend.at[h, to], attin.at[h, head], a_send.at[h, step], a_recv.at[h, step], me, to)

    def each(first, last, action):
        lax.fori_loop(first, last, lambda i, c: (action(i), c)[1], 0)

    def on_core(which, *actions):
        @pl.when(core == which)
        def _():
            for action in actions:
                action()

    barrier = pltpu.get_barrier_semaphore()
    each(1, N_DP, lambda i: pl.semaphore_signal(
        barrier, inc=1, device_id={"dp": (me + i) % N_DP, "seq": sq}, device_id_type=MESH))
    each(1, N_SEQ, lambda i: pl.semaphore_signal(
        barrier, inc=1, device_id={"dp": me, "seq": (sq + i) % N_SEQ}, device_id_type=MESH))

    cols = pl.ds(pl.multiple_of(core * REST, 128), HALF)
    own_w = pltpu.make_async_copy(w, wall.at[v], local.at[0])
    own_p = pltpu.make_async_copy(pw.at[:, cols], pwall.at[core, pu, pv], local.at[1])
    own_w.start()
    own_p.start()

    owners = owner[...]
    owners_f = jnp.broadcast_to(owners.astype(F32), (64, 64))
    owners_col = column_of(owners, 64).astype(F32)
    earlier = (owners_col == owners_f) & (iota((64, 64), 0) < iota((64, 64), 1))
    rank = jnp.sum(jnp.where(earlier, 1.0, 0.0), axis=0, keepdims=True).astype(I32)
    piece_key = out_slot(((owners >> 1) - z + 16) & 15, owners & 1) * 8 + rank * 4
    widen = jnp.where((iota((64, ROWS), 1) >> 2) == iota((64, ROWS), 0), 1.0, 0.0).astype(BF16)
    keys = mm(jnp.broadcast_to(piece_key.astype(F32), (16, 64)).astype(BF16), widen)[0:1].astype(I32)
    keys = keys + (iota((1, ROWS), 1) & 3)
    route_rows = jnp.where(iota((ROWS, ROWS), 0) == keys, 1.0, 0.0).astype(BF16)
    outgoing[...] = mm(route_rows, tok[...]).reshape(N_DP, 8, D).astype(BF16)

    pl.semaphore_wait(barrier, N_DP - 1 + N_SEQ - 1)

    own_w.wait()
    own_p.wait()
    self_in = pltpu.make_async_copy(outgoing.at[core * 16], arrived.at[core], local.at[4])
    self_in.start()
    to_sibling = tok_out((1 - core) * 16)

    each(1, 16, lambda i: tok_out(i).start())
    to_sibling.start()
    for step in (2, 1, 3):
        p_first(step, pv).start()
    on_core(0, lambda: [w_copy(step, v).start() for step in (2, 1, 3)])

    keys_col = column_of(keys, ROWS)
    route[...] = jnp.where(iota((ROWS, ROWS), 1) == keys_col, 1.0, 0.0).astype(BF16)

    def arrival_row(pieces, row):
        source, rank_of = pieces >> 1, pieces & 1
        return in_slot((z - (source >> 1) + 16) & 15, source & 1) * 8 + rank_of * 4 + row

    def table_row(width, clip_shift):
        lane = iota((16, width), 1)
        pick = jnp.where(((lane >> 2) & 15) == iota((16, width), 0), 1.0, 0.0).astype(BF16)
        wide = mm(table[...].astype(F32).astype(BF16), pick)
        mine = (iota((CLIPS, width), 1) >> clip_shift) == iota((CLIPS, width), 0)
        pieces = jnp.sum(jnp.where(mine, wide, 0.0), axis=0, keepdims=True).astype(I32)
        return arrival_row(pieces, iota((1, width), 1) & 3)

    key_short = table_row(ROWS, 6)
    of_clip = iota((ROWS, ROWS), 0) == key_short
    unroute[...] = jnp.where(of_clip, 1.0, 0.0).astype(BF16)
    place = jnp.sum(jnp.where(of_clip, iota((ROWS, ROWS), 1).astype(F32), 0.0), axis=1, keepdims=True)
    clip_col[...] = jnp.broadcast_to(place.astype(I32), (ROWS, 128))
    key_long = table_row(2 * ROWS, 7)
    wide_lane = iota((1, 2 * ROWS), 1)
    key_long = (key_long >> 6) * 128 + ((wide_lane >> 6) & 1) * 64 + (key_long & 63)
    spread[...] = jnp.where(iota((512, 512), 0) == key_long, 1.0, 0.0).astype(BF16)
    spread_t[...] = jnp.where(iota((512, 512), 1) == column_of(key_long, 512), 1.0, 0.0).astype(BF16)

    def of_its_clip(clip, which):
        factors = mod[which].astype(F32)
        rows = [factors[c:c + 1, :] for c in range(CLIPS)]
        return jnp.where(clip == 0, rows[0], jnp.where(clip == 1, rows[1], jnp.where(clip == 2, rows[2], rows[3])))

    def chunk_in(k):
        if k == 0:
            self_in.wait()
            tok_in(1 - core).wait_recv()
        each(k * PER_CHUNK + (2 if k == 0 else 0), (k + 1) * PER_CHUNK, lambda i: tok_in(i).wait_recv())
        rows = arrived[pl.ds(k * PER_CHUNK, PER_CHUNK)].astype(F32).reshape(CHUNK_ROWS, D)
        clip = clip_col[pl.ds(pl.multiple_of(k * CHUNK_ROWS, CHUNK_ROWS), CHUNK_ROWS), 0:1] >> 6
        centered = rows - jnp.mean(rows, axis=-1, keepdims=True)
        variance = jnp.mean(centered * centered, axis=-1, keepdims=True)
        normed = centered * lax.rsqrt(variance + EPSILON)
        hidden = normed * (1.0 + of_its_clip(clip, 1)) + of_its_clip(clip, 0)
        hid[k, pl.ds(u, 1)] = hidden.astype(BF16)[None]
        for step in (2, 1, 3):
            hid_copy(k, step, u).start()

    gains = []
    for i in range(2):
        spread_gain = jnp.broadcast_to(gain[i:i + 1, :], (HD, HD))
        picked = jnp.where(iota((HD, HD), 0) == iota((HD, HD), 1), spread_gain, 0.0)
        gains.append(jnp.sum(picked, axis=1, keepdims=True))

    def own_stage(k):
        return pltpu.make_async_copy(stage.at[k, v], qkv.at[v, k], x_local.at[k])

    def chunk_qkv(k):
        for step in (1, 2, 3):
            hid_copy(k, step, behind(u, step)).wait_recv()
        rows = hid[k].reshape(ROWS, D)
        res[...] = mm_nt(wcat[...], rows)
        for head in range(NX):
            base = head * 3 * HD
            for part in range(2):
                block = res[base + part * HD:base + (part + 1) * HD, :]
                mean_square = jnp.mean(block * block, axis=0, keepdims=True)
                stage[k, head, part] = (block * lax.rsqrt(mean_square + EPSILON) * gains[part]).astype(BF16)
            stage[k, head, 2] = res[base + 2 * HD:base + 3 * HD, :].astype(BF16)
        for step in (2, 1, 3):
            x_copy(k, step, v).start()
        own_stage(k).start()

    def second_batch():
        each(17, N_DP, lambda i: tok_out(i).start())

    def rest_of_projection():
        for step in (1, 2, 3):
            p_first(step, behind(pv, step)).wait_recv()
        for step in (2, 1, 3):
            p_second(step, pu).start()

    def hand_over():
        for step in (1, 2, 3):
            p_second(step, behind(pu, step)).wait_recv()
        each(0, 4, lambda i: p_forward(i, core).start())

    on_core(1, lambda: each(1, 16, lambda i: tok_out(i).wait_send()), second_batch)
    chunk_in(0)
    on_core(0, second_batch)

    def weights_in():
        for step in (1, 2, 3):
            w_copy(step, behind(v, step)).wait_recv()
            w_forward(step).start()

    chunk_in(1)
    on_core(0, weights_in, rest_of_projection)
    chunk_in(2)
    chunk_in(3)
    on_core(1, rest_of_projection)

    on_core(1, lambda: [w_forward(step).wait_recv() for step in (1, 2, 3)])
    for pair in range(2):
        rows = wall[2 * pair:2 * pair + 2].astype(F32).reshape(6 * HD, D)
        wcat[pair * 6 * HD:(pair + 1) * 6 * HD, :] = rows.astype(BF16)
    chunk_qkv(0)
    chunk_qkv(1)
    chunk_qkv(2)
    chunk_qkv(3)
    on_core(0, hand_over)

    for k in range(CHUNKS):
        own_stage(k).wait()
        for step in (1, 2, 3):
            x_copy(k, step, behind(v, step)).wait_recv()
    lane = iota((1, 128), 1)

    def to_clips(col, carry):
        for pair in range(2):
            def part_of(part):
                blocks = [qkv[col, k, part, :, pair * 128:(pair + 1) * 128] for k in range(CHUNKS)]
                return jnp.concatenate(blocks, axis=1)
            queries = mm(part_of(0), spread[...]).astype(BF16)
            keys_of = mm_nt(spread_t[...], part_of(1)).astype(BF16)
            values = mm(part_of(2), spread[...])
            for clip in range(CLIPS):
                cut = slice(clip * 128, (clip + 1) * 128)
                qc[clip, col * 2 + pair] = queries[:, cut]
                kc[clip, col * 2 + pair] = keys_of[cut, :]
                holder = jnp.where(lane < 64, seq_at(pair * 2, col), seq_at(pair * 2 + 1, col))
                position = ((lane >> 2) & 15) * 64 + holder * 4 + (lane & 3)
                inside = jnp.where(position < length[0, clip], 1.0, 0.0)
                ones = jnp.broadcast_to(inside, (8, 128))
                vc[clip, col * 2 + pair] = jnp.concatenate([values[:, cut] * inside, ones], axis=0).astype(BF16)
        return carry

    on_core(1, hand_over)
    lax.fori_loop(0, NX, to_clips, 0)

    factor = math.log2(math.e) / math.sqrt(HD)

    def attend(clip, carry):
        keys_of = kc[clip].reshape(8 * 128, HD)
        values = jnp.concatenate([vc[clip, j] for j in range(8)], axis=1)
        for block in range(4):
            queries = jnp.concatenate([qc[clip, 2 * block], qc[clip, 2 * block + 1]], axis=1)
            scores = mm(keys_of, queries)
            unscaled = jnp.exp2(scores * factor).astype(BF16)
            summed = mm(values, unscaled)
            attended = (summed[0:HD] / summed[HD:HD + 1]).astype(BF16)
            att[clip, 2 * block] = attended[:, 0:128]
            att[clip, 2 * block + 1] = attended[:, 128:256]
        return carry


    come = iota((256, 256), 0)
    go = iota((256, 256), 1)
    swap = jnp.where(come == ((go >> 6) & 1) * 128 + (go >> 7) * 64 + (go & 63), 1.0, 0.0).astype(BF16)

    def self_att(h):
        return pltpu.make_async_copy(attsend.at[h, sq], attin.at[h, sq], local.at[2 + h])

    for h in range(2):
        lax.fori_loop(2 * h, 2 * h + 2, attend, 0)
        for pair in range(8):
            blocks = jnp.concatenate([att[2 * h, pair], att[2 * h + 1, pair]], axis=1)
            swapped = mm(blocks, swap).astype(BF16)
            for half in range(2):
                attsend[h, ((pair % 2) * 2 + half) * 4 + pair // 2] = swapped[:, half * 128:(half + 1) * 128]
        each(1, N_SEQ, lambda i: a_copy(h, i, sq).start())
        self_att(h).start()

    each(0, 4, lambda i: p_forward(i, 1 - core).wait_recv())
    for pair in range(N_SEQ // 2):
        rows = pl.ds(pair * 2 * HD, 2 * HD)
        row, col = pair // 2, (pair % 2) * 2
        left = jnp.concatenate([pwall[0, col, row].astype(F32), pwall[0, col + 1, row].astype(F32)], axis=0)
        right = jnp.concatenate([pwall[1, row, col].astype(F32), pwall[1, row, col + 1].astype(F32)], axis=0)
        pwcat[rows, 0:HALF] = left.astype(BF16)
        pwcat[rows, HALF:D] = right[:, HALF - REST:].astype(BF16)

    for h in range(2):
        self_att(h).wait()
        each(1, N_SEQ, lambda i: a_copy(h, i, (sq - i + N_SEQ) % N_SEQ).wait_recv())
    heads = jnp.concatenate([attin[h].astype(F32).reshape(N_SEQ * HD, 128) for h in range(2)], axis=1).astype(BF16)
    for part in range(4):
        part_rows = ROWS // 4
        cut = slice(part * part_rows, (part + 1) * part_rows)
        joined = mm_nt(unroute[cut, :], heads).astype(BF16)
        branch = mm(joined, pwcat[...])
        where = clip_col[cut, 0:1]
        clip = where >> 6
        position = ((where >> 2) & 15) * 64 + sq * 4 + (where & 3)
        limit = jnp.where(clip == 0, length[0, 0], jnp.where(
            clip == 1, length[0, 1], jnp.where(clip == 2, length[0, 2], length[0, 3])))
        rows = arrived[part * 8:(part + 1) * 8].astype(F32).reshape(part_rows, D)
        result = jnp.where(position < limit, rows + of_its_clip(clip, 2) * branch, 0.0)
        ret[part * 8:(part + 1) * 8] = result.reshape(8, 8, D).astype(BF16)
        each(part * 8 + (2 if part == 0 else 0), part * 8 + 8, lambda i: ret_out(i).start())
    ret_out(1 - core).start()
    self_back = pltpu.make_async_copy(ret.at[core], back.at[core * 16], local.at[6])
    self_back.start()

    for step in (1, 2, 3):
        p_first(step, pv).wait_send()
        p_second(step, pu).wait_send()
        for k in range(CHUNKS):
            hid_copy(k, step, u).wait_send()
            x_copy(k, step, v).wait_send()
    @pl.when(core == 0)
    def _():
        each(1, 16, lambda i: tok_out(i).wait_send())
        for step in (1, 2, 3):
            w_copy(step, v).wait_send()
            w_forward(step).wait_send()

    to_sibling.wait_send()
    each(17, N_DP, lambda i: tok_out(i).wait_send())
    each(0, 4, lambda i: p_forward(i, core).wait_send())
    for h in range(2):
        each(1, N_SEQ, lambda i: a_copy(h, i, sq).wait_send())

    self_back.wait()
    ret_in((1 - core) * 16).wait_recv()
    each(1, 16, lambda i: ret_in(i).wait_recv())
    each(17, N_DP, lambda i: ret_in(i).wait_recv())
    returned = back[...].astype(F32).reshape(ROWS, D).astype(BF16)
    out[...] = mm(route[...], returned).astype(BF16)
    ret_out(1 - core).wait_send()
    each(2, N_DP, lambda i: ret_out(i).wait_send())


def body(tokens, slot_owner, clip_pieces, clip_length, modulation, qkv_weight, qk_gain, proj_weight):
    vmem = pl.BlockSpec(memory_space=pltpu.VMEM)
    smem = pl.BlockSpec(memory_space=pltpu.SMEM)
    dma = pltpu.SemaphoreType.DMA
    result = pl.pallas_call(
        kernel,
        out_shape=jax.ShapeDtypeStruct((ROWS, D), BF16),
        in_specs=[vmem, vmem, vmem, smem, vmem, vmem, vmem, vmem],
        out_specs=vmem,
        scratch_shapes=[
            pltpu.VMEM((N_DP, 8, D), BF16),
            pltpu.VMEM((N_DP, 8, D), BF16),
            pltpu.VMEM((CHUNKS, NY, CHUNK_ROWS, D), BF16),
            pltpu.VMEM((NX, 3, HD, D), BF16),
            pltpu.VMEM((NX * 3 * HD, D), BF16),
            pltpu.VMEM((NX * 3 * HD, ROWS), F32),
            pltpu.VMEM((2, 4, 4, HD, HALF), BF16),
            pltpu.VMEM((N_SEQ * HD, D), BF16),
            pltpu.VMEM((CHUNKS, NX, 3, HD, ROWS), BF16),
            pltpu.VMEM((NX, CHUNKS, 3, HD, ROWS), BF16),
            pltpu.VMEM((CLIPS, 8, HD, 128), BF16),
            pltpu.VMEM((CLIPS, 8, 128, HD), BF16),
            pltpu.VMEM((CLIPS, 8, HD + 8, 128), BF16),
            pltpu.VMEM((CLIPS, 8, HD, 128), BF16),
            pltpu.VMEM((2, N_SEQ, HD, 128), BF16),
            pltpu.VMEM((2, N_SEQ, HD, 128), BF16),
            pltpu.VMEM((N_DP, 8, D), BF16),
            pltpu.VMEM((N_DP, 8, D), BF16),
            pltpu.VMEM((512, 512), BF16),
            pltpu.VMEM((512, 512), BF16),
            pltpu.VMEM((ROWS, ROWS), BF16),
            pltpu.VMEM((ROWS, ROWS), BF16),
            pltpu.VMEM((ROWS, 128), I32),
            dma((N_DP,)), dma((N_DP,)),
            dma((CHUNKS, 4)), dma((CHUNKS, 4)), dma((CHUNKS, 4)), dma((CHUNKS, 4)),
            dma((4,)), dma((4,)), dma((4,)), dma((4,)),
            dma((2, 4)), dma((2, 4)), dma((4,)), dma((4,)), dma((2, N_SEQ)), dma((2, N_SEQ)),
            dma((N_DP,)), dma((N_DP,)),
            dma((8,)), dma((CHUNKS,)),
        ],
        compiler_params=pltpu.CompilerParams(
            collective_id=0, has_side_effects=True, vmem_limit_bytes=50 * 1024 * 1024
        ),
        cost_estimate=pl.CostEstimate(flops=5 * 10**9, bytes_accessed=4 * 10**6, transcendentals=4 * 10**6),
        name="block",
    )(
        tokens[0].reshape(ROWS, D),
        slot_owner,
        clip_pieces[0],
        clip_length,
        modulation[0].transpose(1, 0, 2),
        qkv_weight.transpose(1, 2, 0),
        qk_gain,
        proj_weight,
    )
    return result.reshape(1, 64, 4, D)


def solution(mesh):
    return jax.shard_map(
        body,
        mesh=mesh,
        in_specs=(
            P("dp", None, "seq", None),
            P("dp", None),
            P("dp", None, None),
            P("dp", None),
            P("dp", None, None, None),
            P(None, None, "seq"),
            P(),
            P("seq", None),
        ),
        out_specs=P("dp", None, "seq", None),
        check_vma=False,
    )
```
